32 devices in a mesh: dp: 8 (over z, y), tensor: 4 (over x, core).
Axes of the slice: x: 2, y: 2, z: 4, core: 2. Of those that a mesh axis runs over, the one named last changes fastest.
Arguments:
- policy_rows: bfloat16 [4096, 2048], P('dp'), may hold values from -6 to 6
- frozen_rows: bfloat16 [4096, 2048], P('dp'), may hold values from -6 to 6
- next_tokens: int32 [8, 256], replicated, may hold values from 0 to 50303
- desirable: int32 [8], replicated, may hold values 0 or 1
- answer_len: int32 [8], replicated, may hold values from 64 to 256, as said below
- partner: int32 [8], replicated, may hold values from 0 to 7, each once
- norms_copy: bfloat16 [4, 2048], P(None, 'dp')
- attend_in_copy: bfloat16 [3, 2048, 2048], P(None, 'dp', 'tensor'), may hold values from -0.125 to 0.125
- attend_out_copy: bfloat16 [2048, 2048], P('tensor', 'dp'), may hold values from -2 to 2
- expand_copy: bfloat16 [2048, 8192], P('dp', 'tensor'), may hold values from -0.125 to 0.125
- contract_copy: bfloat16 [8192, 2048], P('tensor', 'dp'), may hold values from -0.0625 to 0.0625
- norms_master: float32 [4, 2048], P(None, 'dp')
- attend_in_master: float32 [3, 2048, 2048], P(None, 'dp', 'tensor'), may hold values from -0.125 to 0.125
- attend_out_master: float32 [2048, 2048], P('tensor', 'dp'), may hold values from -2 to 2
- expand_master: float32 [2048, 8192], P('dp', 'tensor'), may hold values from -0.125 to 0.125
- contract_master: float32 [8192, 2048], P('tensor', 'dp'), may hold values from -0.0625 to 0.0625
- norms_first: float32 [4, 2048], P(None, 'dp'), may hold values from -0.015625 to 0.015625
- attend_in_first: float32 [3, 2048, 2048], P(None, 'dp', 'tensor'), may hold values from -0.0068359375 to 0.0068359375
- attend_out_first: float32 [2048, 2048], P('tensor', 'dp'), may hold values from -0.0008544922 to 0.0008544922
- expand_first: float32 [2048, 8192], P('dp', 'tensor'), may hold values from -0.0008544922 to 0.0008544922
- contract_first: float32 [8192, 2048], P('tensor', 'dp'), may hold values from -0.001953125 to 0.001953125
- norms_second: float32 [4, 2048], P(None, 'dp'), may hold values from 5.4931643e-06 to 2.166748e-05
- attend_in_second: float32 [3, 2048, 2048], P(None, 'dp', 'tensor'), may hold values from 8.087158e-07 to 3.2043456e-06
- attend_out_second: float32 [2048, 2048], P('tensor', 'dp'), may hold values from 2.4414062e-09 to 9.765625e-09
- expand_second: float32 [2048, 8192], P('dp', 'tensor'), may hold values from 1.953125e-09 to 7.8125e-09
- contract_second: float32 [8192, 2048], P('tensor', 'dp'), may hold values from 1.2207031e-08 to 4.8828124e-08
- frozen_norms: float32 [4, 2048], replicated
- frozen_in: bfloat16 [3, 2048, 2048], P(None, None, 'tensor'), may hold values from -0.125 to 0.125
- frozen_out: bfloat16 [2048, 2048], P('tensor'), may hold values from -2 to 2
- frozen_expand: bfloat16 [2048, 8192], P(None, 'tensor'), may hold values from -0.125 to 0.125
- frozen_contract: bfloat16 [8192, 2048], P('tensor'), may hold values from -0.0625 to 0.0625
- vocab_table: bfloat16 [2048, 50304], P(None, 'tensor')
Outputs:
- mixed: bfloat16 [4096, 2048], P('dp')
- input_grad: float32 [4096, 2048], P('dp')
- loss: float32 [1], replicated
- norms_next: float32 [4, 2048], P(None, 'dp')
- attend_in_next: float32 [3, 2048, 2048], P(None, 'dp', 'tensor')
- attend_out_next: float32 [2048, 2048], P('tensor', 'dp')
- expand_next: float32 [2048, 8192], P('dp', 'tensor')
- contract_next: float32 [8192, 2048], P('tensor', 'dp')
- norms_first_next: float32 [4, 2048], P(None, 'dp')
- attend_in_first_next: float32 [3, 2048, 2048], P(None, 'dp', 'tensor')
- attend_out_first_next: float32 [2048, 2048], P('tensor', 'dp')
- expand_first_next: float32 [2048, 8192], P('dp', 'tensor')
- contract_first_next: float32 [8192, 2048], P('tensor', 'dp')
- norms_second_next: float32 [4, 2048], P(None, 'dp')
- attend_in_second_next: float32 [3, 2048, 2048], P(None, 'dp', 'tensor')
- attend_out_second_next: float32 [2048, 2048], P('tensor', 'dp')
- expand_second_next: float32 [2048, 8192], P('dp', 'tensor')
- contract_second_next: float32 [8192, 2048], P('tensor', 'dp')
The draws below stay inside these ranges and needn't reach their ends.
Inputs may be any that keep to these rules, and one draw needn't show every extreme that they name: 1 marks a desirable completion, 0 an undesirable one. `answer_len`: one example has 256 tokens in its completion and another 256 // 4. `partner`: a permutation of the examples.
All inputs are finite; a program needn't handle non-finite values.
Results may differ from the reference program's by a relative error of at most 0.02.
Values may be sent and summed in bfloat16 or wider, within the bound.
A program may use at most 384 MiB of HBM per device.

```python
import math
import jax
import jax.numpy as jnp
import numpy as np
from jax import lax

D = 2048
HEADS = 16
HD = 128
ROT = 32
FF = 8192
VOCAB = 50304
HALF = 256
STEP = 10
EXAMPLES = 8
TOKENS = 4096
N_DP = 8


def norm_rows(key):
    noise = jax.random.normal(key, (4, D), jnp.float32)
    centre = jnp.array([1.0, 0.0, 1.0, 0.0], jnp.float32)[:, None]
    spread = jnp.array([0.15, 0.3, 0.15, 0.3], jnp.float32)[:, None]
    return centre + spread * noise


def draw_norms_copy(key, part):
    key = jax.random.fold_in(key, 3)
    return norm_rows(key).astype(jnp.bfloat16)


def draw_norms_master(key, part):
    key = jax.random.fold_in(key, 5)
    return norm_rows(key)


def draw_frozen_norms(key, part):
    key = jax.random.fold_in(key, 7)
    return norm_rows(key)


def draw_answer_len(key, part):
    key = jax.random.fold_in(key, 13)
    pick_key, length_key = jax.random.split(key)
    lengths = jax.random.randint(length_key, (EXAMPLES,), HALF // 4, HALF + 1, dtype=jnp.int32)
    order = jax.random.permutation(pick_key, EXAMPLES)
    lengths = lengths.at[order[0]].set(HALF)
    lengths = lengths.at[order[1]].set(HALF // 4)
    return lengths.astype(jnp.int32)


def draw_vocab_table(key, part):
    key = jax.random.fold_in(key, 11)
    columns = jnp.arange(VOCAB, dtype=jnp.float32) / VOCAB
    base = jax.random.normal(key, (D, VOCAB), jnp.float32)
    scale = 1.0 + 2.0 * columns
    return (base * scale[None, :] * D ** (-0.5)).astype(jnp.bfloat16)


def touch_ends(values, own_key, smallest, high):
    shape = values.shape
    spot = [jax.random.randint(jax.random.fold_in(own_key, axis), (), 0, shape[axis]) for axis in range(len(shape))]
    values = values.at[tuple(spot)].set(smallest)
    longest = shape.index(max(shape))
    spot[longest] = (spot[longest] + 1) % shape[longest]
    return values.at[tuple(spot)].set(high)


def block_levels(rng, extent, cuts, low, top_value):
    level = 1.0
    for dim, blocks in cuts:
        steps = jax.random.uniform(jax.random.fold_in(jax.random.fold_in(rng, 6), dim), (blocks,), jnp.float32, low / len(cuts), top_value / len(cuts))
        level = level * jnp.repeat(jnp.exp(steps), extent[dim] // blocks).reshape((-1,) + (1,) * (len(extent) - 1 - dim))
    return level


def rank_table(number_of, skew):
    weights = [(1 << 20) // math.isqrt(standing ** skew) + 1 for standing in range(1, number_of + 1)]
    width = 1 + sum(weights) // (1 << 30)
    return np.cumsum(np.array([max(1, weight // width) for weight in weights]))


def skewed_ids(stream_key, extent, amount, lean):
    table = rank_table(amount, lean)
    pick = jax.random.randint(jax.random.fold_in(stream_key, 1), extent, 0, int(table[amount - 1]))
    grade = jnp.searchsorted(jnp.asarray(table, jnp.int32), pick, side="right")
    return jax.random.permutation(jax.random.fold_in(stream_key, 2), amount)[grade].astype(jnp.int32)


def gaussian(own_key, shape, deviation, bound, cuts=(), kind=jnp.bfloat16):
    values = deviation * jax.random.normal(own_key, shape, jnp.float32)
    if cuts:
        values = values * block_levels(own_key, shape, cuts, -0.22, 0.18)
    return jnp.clip(values, -bound, bound).astype(kind)


def setup_inputs(seed: int = 0) -> dict:
    key_of = jax.random.split(jax.random.key(seed), 33)
    policy_rows = gaussian(key_of[0], (TOKENS, D), 1.0, 6.0, ((0, 8),))
    frozen_rows = gaussian(key_of[1], (TOKENS, D), 1.0, 6.0, ((0, 8),))
    next_tokens = touch_ends(skewed_ids(key_of[2], (EXAMPLES, HALF), VOCAB, 2), jax.random.fold_in(key_of[2], 3), 0, VOCAB - 1).astype(jnp.int32)
    desirable = touch_ends((jax.random.randint(key_of[3], (EXAMPLES,), 0, 2) < 1).astype(jnp.int32), jax.random.fold_in(key_of[3], 1), 0, 1)
    answer_len = draw_answer_len(jax.random.fold_in(key_of[32], 71), 0)
    partner = jax.random.permutation(key_of[5], EXAMPLES).astype(jnp.int32)
    norms_copy = draw_norms_copy(jax.random.fold_in(key_of[32], 71), 0)
    attend_in_copy = gaussian(key_of[7], (3, D, D), D ** -0.5, 0.125, ((1, 8), (2, 4)))
    attend_out_copy = gaussian(key_of[8], (D, D), (max(D // HALF, 1)) ** -0.5, 2.0, ((0, 4), (1, 8)))
    expand_copy = gaussian(key_of[9], (D, FF), D ** -0.5, 0.125, ((0, 8), (1, 4)))
    contract_copy = gaussian(key_of[10], (FF, D), FF ** -0.5, 0.0625, ((0, 4), (1, 8)))
    norms_master = draw_norms_master(jax.random.fold_in(key_of[32], 71), 0)
    attend_in_master = gaussian(key_of[12], (3, D, D), D ** -0.5, 0.125, ((1, 8), (2, 4)), jnp.float32)
    attend_out_master = gaussian(key_of[13], (D, D), (max(D // HALF, 1)) ** -0.5, 2.0, ((0, 4), (1, 8)), jnp.float32)
    expand_master = gaussian(key_of[14], (D, FF), D ** -0.5, 0.125, ((0, 8), (1, 4)), jnp.float32)
    contract_master = gaussian(key_of[15], (FF, D), FF ** -0.5, 0.0625, ((0, 4), (1, 8)), jnp.float32)
    norms_first = gaussian(key_of[16], (4, D), (0.29 * N_DP ** 0.5 * HALF ** -0.5 * D ** -0.5), 0.015625, ((1, 8),), jnp.float32)
    attend_in_first = gaussian(key_of[17], (3, D, D), (0.11 * N_DP ** 0.5 * HALF ** -0.5 * D ** -0.5), 0.0068359375, ((1, 8), (2, 4)), jnp.float32)
    attend_out_first = gaussian(key_of[18], (D, D), (0.015 * N_DP ** 0.5 * HALF ** -0.5 * D ** -0.5), 0.0008544922, ((0, 4), (1, 8)), jnp.float32)
    expand_first = gaussian(key_of[19], (D, FF), (0.014 * N_DP ** 0.5 * HALF ** -0.5 * D ** -0.5), 0.0008544922, ((0, 8), (1, 4)), jnp.float32)
    contract_first = gaussian(key_of[20], (FF, D), (0.035 * N_DP ** 0.5 * HALF ** -0.5 * D ** -0.5), 0.001953125, ((0, 4), (1, 8)), jnp.float32)
    norms_second = jnp.clip(jnp.exp(math.log(2.1667479813913815e-05) - 1.372308 * jax.random.uniform(key_of[21], (4, D), jnp.float32) ** block_levels(key_of[21], (4, D), ((1, 8),), -0.2, 0.2)), 5.4931642807787284e-06, 2.1667479813913815e-05)
    attend_in_second = jnp.clip(jnp.exp(math.log(3.204345603080583e-06) - 1.3768156 * jax.random.uniform(key_of[22], (3, D, D), jnp.float32) ** block_levels(key_of[22], (3, D, D), ((1, 8), (2, 4)), -0.2, 0.2)), 8.087158107628056e-07, 3.204345603080583e-06)
    attend_out_second = jnp.clip(jnp.exp(math.log(9.765624753299562e-09) - 1.3862944 * jax.random.uniform(key_of[23], (D, D), jnp.float32) ** block_levels(key_of[23], (D, D), ((0, 4), (1, 8)), -0.2, 0.2)), 2.4414061883248905e-09, 9.765624753299562e-09)
    expand_second = jnp.clip(jnp.exp(math.log(7.812499980275334e-09) - 1.3862944 * jax.random.uniform(key_of[24], (D, FF), jnp.float32) ** block_levels(key_of[24], (D, FF), ((0, 8), (1, 4)), -0.2, 0.2)), 1.9531249950688334e-09, 7.812499980275334e-09)
    contract_second = jnp.clip(jnp.exp(math.log(4.882812376649781e-08) - 1.3862944 * jax.random.uniform(key_of[25], (FF, D), jnp.float32) ** block_levels(key_of[25], (FF, D), ((0, 4), (1, 8)), -0.2, 0.2)), 1.2207030941624453e-08, 4.882812376649781e-08)
    frozen_norms = draw_frozen_norms(jax.random.fold_in(key_of[32], 71), 0)
    frozen_in = gaussian(key_of[27], (3, D, D), D ** -0.5, 0.125, ((2, 4),))
    frozen_out = gaussian(key_of[28], (D, D), (max(D // HALF, 1)) ** -0.5, 2.0, ((0, 4),))
    frozen_expand = gaussian(key_of[29], (D, FF), D ** -0.5, 0.125, ((1, 4),))
    frozen_contract = gaussian(key_of[30], (FF, D), FF ** -0.5, 0.0625, ((0, 4),))
    vocab_table = draw_vocab_table(jax.random.fold_in(key_of[32], 71), 0)
    return dict(policy_rows=policy_rows, frozen_rows=frozen_rows, next_tokens=next_tokens, desirable=desirable, answer_len=answer_len, partner=partner, norms_copy=norms_copy, attend_in_copy=attend_in_copy, attend_out_copy=attend_out_copy, expand_copy=expand_copy, contract_copy=contract_copy, norms_master=norms_master, attend_in_master=attend_in_master, attend_out_master=attend_out_master, expand_master=expand_master, contract_master=contract_master, norms_first=norms_first, attend_in_first=attend_in_first, attend_out_first=attend_out_first, expand_first=expand_first, contract_first=contract_first, norms_second=norms_second, attend_in_second=attend_in_second, attend_out_second=attend_out_second, expand_second=expand_second, contract_second=contract_second, frozen_norms=frozen_norms, frozen_in=frozen_in, frozen_out=frozen_out, frozen_expand=frozen_expand, frozen_contract=frozen_contract, vocab_table=vocab_table)


NORM_EPSILON = 1e-05
KTO_BETA = 2.0
ADAM_ONE = 0.9
ADAM_TWO = 0.95
ADAM_EPSILON = 1e-08
DECAY_RATE = 0.1
NORM_RATE = 0.3
ROPE_BASE = 10000.0
MASKED = -1e+30
HIGHEST_PRECISION = lax.Precision.HIGHEST

@jax.custom_vjp
def low(v):
    return lax.optimization_barrier(v.astype(jnp.bfloat16)).astype(jnp.float32)

@jax.custom_vjp
def low_back(v):
    return v

def low_keep(v):
    return (low(v), None)

def low_pass(kept, grad):
    return (grad,)

def back_keep(v):
    return (v, None)

def back_low(kept, grad):
    return (low(grad),)
low.defvjp(low_keep, low_pass)
low_back.defvjp(back_keep, back_low)

def normalize(values):
    centre = lax.optimization_barrier(jnp.mean(values, axis=-1, keepdims=True))
    centred = values - centre
    return centred * lax.rsqrt(lax.optimization_barrier(jnp.mean(centred * centred, axis=-1, keepdims=True)) + NORM_EPSILON)

def layout(half):
    position_index = jnp.arange(3 * half, dtype=jnp.int32)
    place = jnp.where(position_index < 2 * half, position_index, position_index - half)
    group = jnp.where(position_index < half, 0, jnp.where(position_index < 2 * half, 1, 2))
    allowed = (place[None, :] <= place[:, None]) & ((group[None, :] == 0) | (group[None, :] == group[:, None]))
    freqs = ROPE_BASE ** (-jnp.arange(ROT // 2, dtype=jnp.float32) * 2.0 / ROT)
    angles = place.astype(jnp.float32)[:, None] * freqs[None, :]
    return (allowed, jnp.cos(angles)[:, None, :], jnp.sin(angles)[:, None, :])

def rotate(heads, cosines, sines):
    first = heads[..., :ROT // 2]
    second = heads[..., ROT // 2:ROT]
    return jnp.concatenate([first * cosines - second * sines, second * cosines + first * sines, heads[..., ROT:]], axis=-1)

def block(rows, norms, attend_in, attend_out, expand, contract, allowed, cosines, sines):
    count = rows.shape[0]
    unit = normalize(rows)
    first_in = low(unit * norms[0] + norms[1])
    second_in = low(unit * norms[2] + norms[3])

    def project(which):
        return low_back(jnp.dot(first_in, attend_in[which], precision=HIGHEST_PRECISION)).reshape(count, HEADS, HD)
    query = low(rotate(project(0), cosines, sines))
    keys = low(rotate(project(1), cosines, sines))
    values = low(project(2))
    scores = low_back(jnp.einsum('qhd,khd->hqk', query, keys, precision=HIGHEST_PRECISION) * HD ** (-0.5))
    scores = jnp.where(allowed[None], scores, MASKED)
    peak = lax.optimization_barrier(jnp.max(scores, axis=-1, keepdims=True))
    raised = jnp.exp(scores - peak)
    chance = low(raised / lax.optimization_barrier(jnp.sum(raised, axis=-1, keepdims=True)))
    attended = low(low_back(jnp.einsum('hqk,khd->qhd', chance, values, precision=HIGHEST_PRECISION))).reshape(count, HEADS * HD)
    hidden = low(jax.nn.gelu(low_back(jnp.dot(second_in, expand, precision=HIGHEST_PRECISION)), approximate=False))
    branch = low_back(jnp.dot(attended, attend_out, precision=HIGHEST_PRECISION) + jnp.dot(hidden, contract, precision=HIGHEST_PRECISION))
    return rows + branch

def log_probs(out_rows, table, targets):
    unit = low(normalize(out_rows))
    logits = low_back(jnp.dot(unit, table, precision=HIGHEST_PRECISION))
    peak = lax.optimization_barrier(jnp.max(logits, axis=-1, keepdims=True))
    log_total = peak[:, 0] + jnp.log(lax.optimization_barrier(jnp.sum(jnp.exp(logits - peak), axis=-1)))
    picked = jnp.take_along_axis(logits, targets[:, None], axis=1)[:, 0]
    return picked - log_total

def example_logp(position, rows_all, next_tokens, partner, params, table, allowed, cosines, sines):
    other = partner[position]
    own_rows = lax.dynamic_index_in_dim(rows_all, position, 0, keepdims=False)
    other_rows = lax.dynamic_index_in_dim(rows_all, other, 0, keepdims=False)
    rows = jnp.concatenate([own_rows, other_rows[HALF:]], axis=0)
    out = block(rows, params[0], params[1], params[2], params[3], params[4], allowed, cosines, sines)
    targets = jnp.concatenate([next_tokens[position], next_tokens[other]])
    return (log_probs(out[HALF:], table, targets), out[:2 * HALF])

def adamw_step(master, first, second, gradient, rate, decay):
    new_first = ADAM_ONE * first + (1.0 - ADAM_ONE) * gradient
    new_second = ADAM_TWO * second + (1.0 - ADAM_TWO) * gradient * gradient
    ratio = new_first / (1.0 - ADAM_ONE ** STEP) / (jnp.sqrt(new_second / (1.0 - ADAM_TWO ** STEP)) + ADAM_EPSILON)
    return (master - rate * (ratio + decay * master), new_first, new_second)

def reference(policy_rows, frozen_rows, next_tokens, desirable, answer_len, partner, norms_copy, attend_in_copy, attend_out_copy, expand_copy, contract_copy, norms_master, attend_in_master, attend_out_master, expand_master, contract_master, norms_first, attend_in_first, attend_out_first, expand_first, contract_first, norms_second, attend_in_second, attend_out_second, expand_second, contract_second, frozen_norms, frozen_in, frozen_out, frozen_expand, frozen_contract, vocab_table):
    allowed, cosines, sines = layout(HALF)
    table = vocab_table.astype(jnp.float32)
    frozen_params = (frozen_norms, frozen_in.astype(jnp.float32), frozen_out.astype(jnp.float32), frozen_expand.astype(jnp.float32), frozen_contract.astype(jnp.float32))
    indices = jnp.arange(EXAMPLES, dtype=jnp.int32)
    frozen_all = frozen_rows.astype(jnp.float32).reshape(EXAMPLES, 2 * HALF, D)
    frozen_logp, unused = lax.map(lambda position: example_logp(position, frozen_all, next_tokens, partner, frozen_params, table, allowed, cosines, sines), indices)
    steps = jnp.arange(HALF, dtype=jnp.int32)
    other_len = answer_len[partner]
    own_live = (steps[None, :] < answer_len[:, None]).astype(jnp.float32)
    other_live = (steps[None, :] < other_len[:, None]).astype(jnp.float32)
    own_count = answer_len.astype(jnp.float32)
    other_count = other_len.astype(jnp.float32)

    def sequence_means(logp):
        return (lax.optimization_barrier(jnp.sum(logp[:, :HALF] * own_live, axis=1)) / own_count, lax.optimization_barrier(jnp.sum(logp[:, HALF:] * other_live, axis=1)) / other_count)
    frozen_own, frozen_other = sequence_means(frozen_logp)
    sign = (2 * desirable - 1).astype(jnp.float32)

    def objective(params, rows):
        rows_all = rows.reshape(EXAMPLES, 2 * HALF, D)
        one = jax.checkpoint(lambda position: example_logp(position, rows_all, next_tokens, partner, params, table, allowed, cosines, sines))
        logp, outputs = lax.map(one, indices)
        policy_own, policy_other = sequence_means(logp)
        drift = jnp.mean(policy_other - frozen_other)
        penalty = jax.nn.softplus(drift)
        total_loss = jnp.sum(1.0 - jax.nn.sigmoid(KTO_BETA * sign * (policy_own - frozen_own - penalty)))
        return (total_loss, outputs.reshape(EXAMPLES * 2 * HALF, D))
    params = (norms_copy.astype(jnp.float32), attend_in_copy.astype(jnp.float32), attend_out_copy.astype(jnp.float32), expand_copy.astype(jnp.float32), contract_copy.astype(jnp.float32))
    total_loss, pull_back, outputs = jax.vjp(objective, params, policy_rows.astype(jnp.float32), has_aux=True)
    param_grads, row_grads = pull_back(jnp.ones_like(total_loss))
    matrix_rate = 0.5 * D ** (-0.5)
    out_rate = 0.5 * max(D // HALF, 1) ** (-0.5)
    masters = (norms_master, attend_in_master, attend_out_master, expand_master, contract_master)
    firsts = (norms_first, attend_in_first, attend_out_first, expand_first, contract_first)
    seconds = (norms_second, attend_in_second, attend_out_second, expand_second, contract_second)
    rates = (NORM_RATE, matrix_rate, out_rate, matrix_rate, matrix_rate)
    decays = (0.0, DECAY_RATE, DECAY_RATE, DECAY_RATE, DECAY_RATE)
    updated = [adamw_step(master, first, second, gradient, rate, decay) for master, first, second, gradient, rate, decay in zip(masters, firsts, seconds, param_grads, rates, decays)]
    return (outputs.astype(jnp.bfloat16), row_grads, jnp.reshape(total_loss, (1,)), updated[0][0], updated[1][0], updated[2][0], updated[3][0], updated[4][0], updated[0][1], updated[1][1], updated[2][1], updated[3][1], updated[4][1], updated[0][2], updated[1][2], updated[2][2], updated[3][2], updated[4][2])
```

```python
import jax
import jax.numpy as jnp
from jax import lax
from jax.experimental import pallas as pl
from jax.experimental.pallas import tpu as pltpu
from jax.sharding import PartitionSpec as P

D = 2048
HD = 128
ROT = 32
HALF = 256
STEP = 10


NORM_EPSILON = 1e-05
KTO_BETA = 2.0
ADAM_ONE = 0.9
ADAM_TWO = 0.95
ADAM_EPSILON = 1e-08
DECAY_RATE = 0.1
NORM_RATE = 0.3
ROPE_BASE = 10000.0
MASKED = -1e30

BF = jnp.bfloat16
F32 = jnp.float32


def dot(a, b, dims):
    return lax.dot_general(a, b, (dims, ((), ())), preferred_element_type=F32)


NN = ((1,), (0,))
NT = ((1,), (1,))
TN = ((0,), (0,))


def dp_shape():
    groups = lax.axis_size("dp")
    pair = 2 if groups % 2 == 0 else 1
    return groups, pair, groups // pair


def pair_swap(value):
    groups, _, _ = dp_shape()
    return lax.ppermute(value, "dp", [(i, i ^ 1) for i in range(groups)])


def dp_place():
    _, pair, _ = dp_shape()
    own = lax.axis_index("dp")
    return own // pair, own % pair


def tensor_swap(value, bit):
    return lax.ppermute(value, "tensor", [(i, i ^ bit) for i in range(lax.axis_size("tensor"))])


def ring_groups():
    _, pair, ring = dp_shape()
    return [[r * pair + p for r in range(ring)] for p in range(pair)]


def gather_ring(piece):
    return lax.all_gather(piece, "dp", axis_index_groups=ring_groups())


def scatter_ring(blocks):
    return lax.psum_scatter(blocks, "dp", axis_index_groups=ring_groups())


def by_side(mine, other, axis):
    _, low = dp_place()
    first, second = jnp.stack([mine, other], axis), jnp.stack([other, mine], axis)
    return jnp.where(low == 0, first, second)


def rows_of(mine, other):
    if other is None:
        return mine
    both = by_side(mine, other, 1)
    return both.reshape((-1,) + both.shape[2:])


def to_ring(kept, came):
    if came is not None:
        kept = (kept.astype(F32) + came.astype(F32)).astype(BF)
    return kept[:, 0]


def columns_of(mine, other):
    both = mine[:, None] if other is None else by_side(mine, other, 1)
    ring, pair, rows, slab = both.shape
    return jnp.moveaxis(both, 2, 0).reshape(rows, ring * pair * slab)


def gather_step(held, bit):
    groups = lax.axis_size("dp")
    came = lax.ppermute(held, "dp", [(i, i ^ bit) for i in range(groups)])
    return jnp.where(
        lax.axis_index("dp") & bit == 0,
        jnp.concatenate([held, came]),
        jnp.concatenate([came, held]),
    )


def gather_small(value):
    groups = lax.axis_size("dp")
    if groups & (groups - 1):
        return lax.all_gather(value, "dp")
    held = value[None]
    bit = 1
    while bit < groups:
        held = gather_step(held, bit)
        bit *= 2
    return held


def sum_small(value, axes):
    for axis in axes:
        size = lax.axis_size(axis)
        if size & (size - 1):
            value = lax.psum(value, axis)
            continue
        bit = 1
        while bit < size:
            value = value + lax.ppermute(value, axis, [(i, i ^ bit) for i in range(size)])
            bit *= 2
    return value


def tensor_near(part):
    low = lax.axis_index("tensor") % 2
    half = part.shape[0] // 2
    kept = lax.dynamic_slice_in_dim(part, low * half, half, 0)
    sent = lax.dynamic_slice_in_dim(part, (1 - low) * half, half, 0)
    return (kept.astype(F32) + tensor_swap(sent, 1).astype(F32)).astype(BF)


def tensor_far(kept):
    return (kept.astype(F32) + tensor_swap(kept, 2).astype(F32)).astype(BF)


def tensor_halves(part):
    part = part.astype(BF)
    if lax.axis_size("tensor") != 4:
        whole = lax.psum(part, "tensor")
        half = part.shape[0] // 2
        return whole[:half], whole[half:], jnp.zeros((1,), jnp.int32)
    kept = tensor_far(tensor_near(part))
    return kept, tensor_swap(kept, 1), (lax.axis_index("tensor") % 2).reshape(1)


def whole_rows(mine, other, low):
    return jnp.where(
        low[0] == 0, jnp.concatenate([mine, other], axis=0), jnp.concatenate([other, mine], axis=0)
    )


def tensor_sum(part):
    return whole_rows(*tensor_halves(part))


def back_columns(pull_logits, table, gaps):
    slices = 4
    step = table.shape[0] // slices
    groups = lax.axis_size("dp")
    product = lambda i: dot(pull_logits, table[i * step : (i + 1) * step], NT).astype(BF)
    if lax.axis_size("tensor") != 4 or groups & (groups - 1):
        return gather_small(gaps), [tensor_halves(product(i)) for i in range(slices)]
    steps = groups.bit_length() - 1
    held, hops = gaps[None], 0
    near, far, parts = [], [], []
    for i in range(slices):
        if i:
            share = -(-steps // (slices - 1))
            for _ in range(min(share, steps - hops)):
                held = gather_step(held, 1 << hops)
                hops += 1
        waits = [pull_logits, held]
        if i >= 2:
            near.append(tensor_near(parts[i - 2]))
            waits.append(near[-1])
        if i >= 3:
            far.append(tensor_far(near[i - 3]))
            waits.append(far[-1])
        waits = lax.optimization_barrier(tuple(waits))
        pull_logits, held = waits[:2]
        if i >= 2:
            near[-1] = waits[2]
        if i >= 3:
            far[-1] = waits[3]
        parts.append(product(i))
    near += [tensor_near(parts[i]) for i in range(slices - 2, slices)]
    far += [tensor_far(near[i]) for i in range(slices - 3, slices)]
    low = (lax.axis_index("tensor") % 2).reshape(1)
    return held, [(kept, tensor_swap(kept, 1), low) for kept in far]


def tensor_join(part):
    if lax.axis_size("tensor") != 4:
        return lax.all_gather(part, "tensor")
    me = lax.axis_index("tensor")
    far = tensor_swap(part, 2)
    two = jnp.where(me // 2 == 0, jnp.stack([part, far]), jnp.stack([far, part]))
    near = tensor_swap(two, 1)
    four = jnp.where(me % 2 == 0, jnp.stack([two, near], 1), jnp.stack([near, two], 1))
    return four.reshape((4,) + part.shape)


def normalize(values):
    centre = jnp.mean(values, axis=-1, keepdims=True)
    centred = values - centre
    inverse_scale = lax.rsqrt(jnp.mean(centred * centred, axis=-1, keepdims=True) + NORM_EPSILON)
    return (centred * inverse_scale, inverse_scale)


def normalize_back(upstream, unit, inverse_scale):
    return inverse_scale * (
        upstream
        - jnp.mean(upstream, axis=-1, keepdims=True)
        - unit * jnp.mean(upstream * unit, axis=-1, keepdims=True)
    )


def after(value, *others):
    return lax.optimization_barrier((value,) + others)[0]


def turn_tables(half):
    place = jnp.arange(3 * half, dtype=jnp.int32)
    place = jnp.where(place < 2 * half, place, place - half)
    freqs = ROPE_BASE ** (-jnp.arange(ROT // 2, dtype=F32) * 2.0 / ROT)
    angles = place.astype(F32)[:, None] * freqs[None, :]
    cosines, sines = jnp.cos(angles), jnp.sin(angles)
    rest = jnp.zeros((3 * half, HD - ROT), F32)
    none = jnp.zeros_like(sines)
    return jnp.stack(
        [
            jnp.concatenate([cosines, cosines, rest + 1.0], axis=1),
            jnp.concatenate([-sines, none, rest], axis=1),
            jnp.concatenate([none, sines, rest], axis=1),
        ]
    )


def turned(x, table, way):
    step = ROT // 2
    moved = pltpu.roll(x, HD - step, 1) * table[1] + pltpu.roll(x, step, 1) * table[2]
    return x * table[0] + moved * way


def seen_scores(query, near, far, half):
    scale = HD ** (-0.5)
    rows = lax.broadcasted_iota(jnp.int32, (half, half), 0)
    cols = lax.broadcasted_iota(jnp.int32, (half, half), 1)
    own = jnp.where(cols <= rows, dot(query, near, NT) * scale, MASKED)
    peak = jnp.max(own, axis=1, keepdims=True)
    if far is None:
        own = jnp.exp(own - peak)
        return own / jnp.sum(own, axis=1, keepdims=True), None
    before = dot(query, far, NT) * scale
    peak = jnp.maximum(peak, jnp.max(before, axis=1, keepdims=True))
    own, before = jnp.exp(own - peak), jnp.exp(before - peak)
    total = jnp.sum(own, axis=1, keepdims=True) + jnp.sum(before, axis=1, keepdims=True)
    return own / total, before / total


def attend_body(half, skip, x_ref, w_ref, t_ref, out_ref, q_ref, k_ref, v_ref):
    x = x_ref[...]
    raw = [dot(x[skip:], w_ref[0], NN), dot(x, w_ref[1], NN), dot(x, w_ref[2], NN)]
    for h in range(w_ref.shape[2] // HD):
        at = slice(h * HD, (h + 1) * HD)
        query = turned(raw[0][:, at], t_ref[:, skip:], 1.0).astype(BF)
        keys = turned(raw[1][:, at], t_ref[...], 1.0).astype(BF)
        values = raw[2][:, at].astype(BF)
        q_ref[:, at], k_ref[:, at], v_ref[:, at] = query, keys, values
        part = lambda x, g, gone=0: x[g * half - gone : (g + 1) * half - gone]
        for g in range(skip // half, 3):
            own, before = seen_scores(
                part(query, g, skip), part(keys, g), part(keys, 0) if g else None, half
            )
            seen = dot(own.astype(BF), part(values, g), NN)
            if g:
                seen = seen + dot(before.astype(BF), part(values, 0), NN)
            out_ref[g * half - skip : (g + 1) * half - skip, at] = seen.astype(BF)


def head_pairs(inner):
    return 2 * HD if inner % (2 * HD) == 0 else HD


def attention(first_in, weights, tables, half, skip):
    count, width = first_in.shape
    inner = weights.shape[2]
    block = head_pairs(inner)
    columns = lambda rows: pl.BlockSpec((rows, block), lambda h: (0, h))
    shape = lambda rows: jax.ShapeDtypeStruct((rows, inner), BF)
    return pl.pallas_call(
        lambda *refs: attend_body(half, skip, *refs),
        grid=(inner // block,),
        in_specs=[
            pl.BlockSpec((count, width), lambda h: (0, 0)),
            pl.BlockSpec((3, width, block), lambda h: (0, 0, h)),
            pl.BlockSpec(tables.shape, lambda h: (0, 0, 0)),
        ],
        out_specs=[columns(count - skip), columns(count - skip), columns(count), columns(count)],
        out_shape=[shape(count - skip), shape(count - skip), shape(count), shape(count)],
        compiler_params=pltpu.CompilerParams(vmem_limit_bytes=48 * 2**20),
        cost_estimate=pl.CostEstimate(
            flops=2 * count * width * inner * 3, bytes_accessed=20 * 2**20, transcendentals=0
        ),
        name="attend",
    )(first_in, weights, tables)


def attend_back_body(half, d_ref, q_ref, k_ref, v_ref, t_ref, out_ref):
    scale = HD ** (-0.5)
    for h in range(d_ref.shape[1] // HD):
        at = slice(h * HD, (h + 1) * HD)
        part = lambda ref, g: ref[g * half : (g + 1) * half, at]
        back_keys = back_values = None
        for g in (1, 2):
            query, far, near = part(q_ref, g), part(k_ref, 0), part(k_ref, g)
            upstream = part(d_ref, g - 1)
            own, before = seen_scores(query, near, far, half)
            own_pull = dot(upstream, part(v_ref, g), NT)
            far_pull = dot(upstream, part(v_ref, 0), NT)
            mean = jnp.sum(own * own_pull, axis=1, keepdims=True) + jnp.sum(
                before * far_pull, axis=1, keepdims=True
            )
            own_back = (own * (own_pull - mean)).astype(BF)
            far_back = (before * (far_pull - mean)).astype(BF)
            back_query = (dot(own_back, near, NN) + dot(far_back, far, NN)) * scale
            rows = slice(g * half, (g + 1) * half)
            out_ref[0, rows, at] = turned(
                back_query, t_ref[:, rows], -1.0
            ).astype(BF)
            out_ref[1, rows, at] = turned(
                dot(own_back, query, TN) * scale, t_ref[:, rows], -1.0
            ).astype(BF)
            out_ref[2, rows, at] = dot(own.astype(BF), upstream, TN).astype(BF)
            more_keys, more_values = dot(far_back, query, TN), dot(before.astype(BF), upstream, TN)
            back_keys = more_keys if back_keys is None else back_keys + more_keys
            back_values = more_values if back_values is None else back_values + more_values
        out_ref[0, :half, at] = jnp.zeros((half, HD), BF)
        out_ref[1, :half, at] = turned(back_keys * scale, t_ref[:, :half], -1.0).astype(BF)
        out_ref[2, :half, at] = back_values.astype(BF)


def attention_back(back_attended, query, keys, values, tables, half):
    count, inner = keys.shape
    block = head_pairs(inner)
    columns = lambda rows: pl.BlockSpec((rows, block), lambda h: (0, h))
    return pl.pallas_call(
        lambda *refs: attend_back_body(half, *refs),
        grid=(inner // block,),
        in_specs=[
            columns(count - half),
            columns(count),
            columns(count),
            columns(count),
            pl.BlockSpec(tables.shape, lambda h: (0, 0, 0)),
        ],
        out_specs=pl.BlockSpec((3, count, block), lambda h: (0, 0, h)),
        out_shape=jax.ShapeDtypeStruct((3, count, inner), BF),
        compiler_params=pltpu.CompilerParams(vmem_limit_bytes=48 * 2**20),
        cost_estimate=pl.CostEstimate(
            flops=2**31, bytes_accessed=8 * 2**20, transcendentals=2**20
        ),
        name="attend_back",
    )(back_attended, query, keys, values, tables)


def hidden_body(skip, x_ref, w_ref, out_ref, *slope_ref):
    before = dot(x_ref[...], w_ref[...], NN)
    share = 0.5 + 0.5 * lax.erf(before * 0.5**0.5)
    out_ref[...] = (before * share).astype(BF)
    if slope_ref:
        kept = before[skip:]
        bell = jnp.exp(-0.5 * kept * kept) * (2.0 * jnp.pi) ** (-0.5)
        slope_ref[0][...] = share[skip:] + kept * bell


def hidden_units(second_in, expand, skip=None):
    count, width = second_in.shape
    units = expand.shape[1]
    block = 256
    column = lambda rows: pl.BlockSpec((rows, block), lambda i: (0, i))
    out_specs, out_shape = [column(count)], [jax.ShapeDtypeStruct((count, units), BF)]
    if skip is not None:
        out_specs.append(column(count - skip))
        out_shape.append(jax.ShapeDtypeStruct((count - skip, units), F32))
    return pl.pallas_call(
        lambda *refs: hidden_body(skip, *refs),
        grid=(units // block,),
        in_specs=[pl.BlockSpec((count, width), lambda i: (0, 0)), column(width)],
        out_specs=out_specs,
        out_shape=out_shape,
        compiler_params=pltpu.CompilerParams(vmem_limit_bytes=48 * 2**20),
        cost_estimate=pl.CostEstimate(
            flops=2 * count * width * units,
            bytes_accessed=2 * width * units + 8 * count * units,
            transcendentals=count * units,
        ),
        name="hidden",
    )(second_in, expand)


def shard_of(r, side, low, pair):
    return r * pair + (low[0] + side) % pair


def grad_body(x_ref, y_ref, out_ref):
    x = x_ref[...]
    for i in range(y_ref.shape[0]):
        out_ref[0, 0, i] = dot(x, y_ref[i], TN).astype(BF)


def grad_blocks(left, right, sides):
    groups, pair, ring = dp_shape()
    low = dp_place()[1].reshape(1)
    rows = left.shape[0]
    slab = left.shape[1] // groups
    parts, _, width = right.shape
    if slab % 128:
        shards = left.reshape(rows, ring, pair, slab)
        shards = jnp.stack([shards[:, :, (low[0] + s) % pair] for s in sides], axis=2)
        out = jnp.einsum("nrsc,pnw->rspcw", shards, right, preferred_element_type=F32)
        return out.astype(BF)
    first = sides[0]
    return pl.pallas_call(
        lambda low_ref, *refs: grad_body(*refs),
        grid_spec=pltpu.PrefetchScalarGridSpec(
            num_scalar_prefetch=1,
            grid=(ring, len(sides)),
            in_specs=[
                pl.BlockSpec((rows, slab), lambda r, s, l: (0, shard_of(r, s + first, l, pair))),
                pl.BlockSpec(right.shape, lambda r, s, l: (0, 0, 0)),
            ],
            out_specs=pl.BlockSpec(
                (1, 1, parts, slab, width), lambda r, s, l: (r, s, 0, 0, 0)
            ),
        ),
        out_shape=jax.ShapeDtypeStruct((ring, len(sides), parts, slab, width), BF),
        compiler_params=pltpu.CompilerParams(vmem_limit_bytes=48 * 2**20),
        cost_estimate=pl.CostEstimate(
            flops=2 * rows * slab * ring * len(sides) * parts * width,
            bytes_accessed=2 * slab * ring * len(sides) * parts * width,
            transcendentals=0,
        ),
        name="grad_blocks",
    )(low, left, right)


def branch_body(pair, x_ref, y_ref, *refs):
    hidden_refs, attend_refs, out_ref = refs[:pair], refs[pair : 2 * pair], refs[-1]

    def write(side):
        out_ref[...] = (
            dot(x_ref[...], hidden_refs[side][0], NN) + dot(y_ref[...], attend_refs[side][0], NN)
        ).astype(BF)

    for side in range(pair):
        pl.when(pl.program_id(1) == side)(lambda: write(side))


def branch_terms(hidden, attended, contract, attend_out, start, count):
    groups, pair, ring = dp_shape()
    low = dp_place()[1].reshape(1)
    slab = contract[0].shape[2]
    if slab % 128:
        rows = slice(start, start + count)
        out = 0.0
        for x, sides in ((hidden[rows], contract), (attended[rows], attend_out)):
            if pair == 2:
                sides = [by_side(sides[0], sides[1], 1)]
            weight = sides[0].reshape(groups, x.shape[1], slab)
            out = out + jnp.einsum("nf,sfc->nsc", x, weight, preferred_element_type=F32)
        return out.reshape(count, groups * slab).astype(BF)
    weights = [*contract[:pair], *attend_out[:pair]]
    units, inner = hidden.shape[1], attended.shape[1]
    return pl.pallas_call(
        lambda low_ref, *refs: branch_body(pair, *refs),
        grid_spec=pltpu.PrefetchScalarGridSpec(
            num_scalar_prefetch=1,
            grid=(ring, pair),
            in_specs=[
                pl.BlockSpec((count, units), lambda r, s, l: (start // count, 0)),
                pl.BlockSpec((count, inner), lambda r, s, l: (start // count, 0)),
                *(pl.BlockSpec((1,) + x.shape[1:], lambda r, s, l: (r, 0, 0)) for x in weights),
            ],
            out_specs=pl.BlockSpec(
                (count, slab), lambda r, s, l: (0, shard_of(r, s, l, pair))
            ),
        ),
        out_shape=jax.ShapeDtypeStruct((count, groups * slab), BF),
        compiler_params=pltpu.CompilerParams(vmem_limit_bytes=48 * 2**20),
        cost_estimate=pl.CostEstimate(
            flops=2 * count * (units + inner) * groups * slab,
            bytes_accessed=2 * (units + inner) * groups * slab,
            transcendentals=0,
        ),
        name="branch",
    )(low, hidden, attended, *weights)


def out_body(x_ref, mine_ref, other_ref, low_ref, unit_ref, low_unit_ref, scale_ref, out_ref):
    mine = pl.program_id(0) == low_ref[0]
    branch = jnp.where(mine, mine_ref[...].astype(F32), other_ref[...].astype(F32))
    out = x_ref[...].astype(F32) + branch
    unit, scale = normalize(out)
    unit_ref[...] = unit
    low_unit_ref[...] = unit.astype(BF)
    scale_ref[...] = scale
    out_ref[...] = out.astype(BF)


def out_rows(x, halves):
    mine, other, low = halves
    rows, width = x.shape
    block = 128
    steps = rows // 2 // block
    whole = pl.BlockSpec((block, width), lambda h, i: (h * steps + i, 0))
    part = pl.BlockSpec((block, width), lambda h, i: (i, 0))
    return pl.pallas_call(
        out_body,
        grid=(2, steps),
        in_specs=[whole, part, part, pl.BlockSpec(memory_space=pltpu.SMEM)],
        out_specs=[whole, whole, pl.BlockSpec((block, 1), lambda h, i: (h * steps + i, 0)), whole],
        out_shape=[
            jax.ShapeDtypeStruct((rows, width), F32),
            jax.ShapeDtypeStruct((rows, width), BF),
            jax.ShapeDtypeStruct((rows, 1), F32),
            jax.ShapeDtypeStruct((rows, width), BF),
        ],
        compiler_params=pltpu.CompilerParams(vmem_limit_bytes=48 * 2**20),
        name="out_rows",
    )(x, mine, other, low)


def borrow_rows(tail, order, *first):
    groups = lax.axis_size("dp")
    parts = lax.axis_size("tensor")
    count, rows, width = tail.shape
    share = rows // parts
    mine = lax.dynamic_slice_in_dim(tail, lax.axis_index("tensor") * share, share, 1)
    mine = mine.reshape(count, groups, share // groups, width).swapaxes(0, 1)
    spread = after(lax.all_to_all(mine, "dp", split_axis=0, concat_axis=0, tiled=True), *first)
    landed = lax.all_to_all(
        jnp.take(spread, order, axis=0), "dp", split_axis=0, concat_axis=0, tiled=True
    )
    landed = landed.swapaxes(0, 1).reshape(count, share, width)
    return tensor_join(landed).swapaxes(0, 1).reshape(count, rows, width)


def head_stats(unit_low, table, local_targets):
    logits = dot(unit_low, table, NN)
    peak = jnp.max(logits, axis=-1)
    total = jnp.sum(jnp.exp(logits - peak[:, None]), axis=-1)
    target_hit = jnp.arange(table.shape[1], dtype=jnp.int32)[None, :] == local_targets[:, None]
    picked = jnp.sum(jnp.where(target_hit, logits, 0.0), axis=-1)
    return jnp.stack([peak, total, picked]), logits, target_hit


def join_stats(stats):
    every = lax.all_gather(stats, "tensor")
    peak = jnp.max(every[:, 0], axis=0)
    total = jnp.sum(every[:, 1] * jnp.exp(every[:, 0] - peak[None]), axis=0)
    return peak, total, jnp.sum(every[:, 2], axis=0)


def adamw_step(master, first, second, gradient, rate, decay):
    new_first = ADAM_ONE * first + (1.0 - ADAM_ONE) * gradient
    new_second = ADAM_TWO * second + (1.0 - ADAM_TWO) * gradient * gradient
    ratio = (
        new_first
        / (1.0 - ADAM_ONE**STEP)
        / (jnp.sqrt(new_second / (1.0 - ADAM_TWO**STEP)) + ADAM_EPSILON)
    )
    return (master - rate * (ratio + decay * master), new_first, new_second)


def per_device(
    policy_rows,
    frozen_rows,
    next_tokens,
    desirable,
    answer_len,
    partner,
    norms_copy,
    attend_in_copy,
    attend_out_copy,
    expand_copy,
    contract_copy,
    norms_master,
    attend_in_master,
    attend_out_master,
    expand_master,
    contract_master,
    norms_first,
    attend_in_first,
    attend_out_first,
    expand_first,
    contract_first,
    norms_second,
    attend_in_second,
    attend_out_second,
    expand_second,
    contract_second,
    frozen_norms,
    frozen_in,
    frozen_out,
    frozen_expand,
    frozen_contract,
    vocab_table,
):
    groups = lax.axis_size("dp")
    own_index = lax.axis_index("dp")
    half = policy_rows.shape[0] // 2
    inner = attend_in_copy.shape[2]
    slab = attend_in_copy.shape[1]
    width = policy_rows.shape[1]
    inverse = jnp.zeros_like(partner).at[partner].set(jnp.arange(groups, dtype=jnp.int32))
    other_index = partner[own_index]

    norms_full = gather_small(norms_copy).swapaxes(0, 1).reshape(4, width).astype(F32)
    units = expand_copy.shape[1]
    _, pair, ring = dp_shape()
    _, low = dp_place()
    swap = pair_swap if pair == 2 else (lambda value: None)
    cut = (units + inner) // 2
    out_came = swap(attend_out_copy)
    attend_mine = gather_ring(attend_in_copy)
    expand_mine = gather_ring(expand_copy)
    contract_mine = gather_ring(contract_copy)
    out_mine = gather_ring(attend_out_copy)
    out_other = None if out_came is None else gather_ring(out_came)

    other = borrow_rows(jnp.stack([frozen_rows[half:], policy_rows[half:]]), partner)
    tables = turn_tables(half)

    frozen_work = jnp.concatenate([frozen_rows, other[0]], axis=0).astype(F32)
    frozen_unit, _ = normalize(frozen_work)
    frozen_first_in = (frozen_unit * frozen_norms[0] + frozen_norms[1]).astype(BF)
    frozen_second_in = (frozen_unit[half:] * frozen_norms[2] + frozen_norms[3]).astype(BF)
    frozen_first_in, frozen_second_in, attend_mine = lax.optimization_barrier(
        (frozen_first_in, frozen_second_in, attend_mine)
    )
    attend_other = swap(attend_mine)
    frozen_attended = attention(frozen_first_in, frozen_in, tables, half, half)[0]
    (frozen_hidden,) = hidden_units(frozen_second_in, frozen_expand)
    frozen_part = dot(frozen_attended, frozen_out, NN) + dot(frozen_hidden, frozen_contract, NN)
    frozen_part, attend_other, expand_mine = lax.optimization_barrier(
        (frozen_part.astype(BF), attend_other, expand_mine)
    )
    expand_other = swap(expand_mine)
    frozen_low = out_rows(
        jnp.concatenate([frozen_rows[half:], other[0]], axis=0), tensor_halves(frozen_part)
    )[1]
    vocab_local = vocab_table.shape[1]
    targets = (
        jnp.concatenate([next_tokens[own_index], next_tokens[other_index]])
        - lax.axis_index("tensor") * vocab_local
    )
    work = jnp.concatenate([policy_rows, other[1]], axis=0).astype(F32)
    unit, inverse_scale = normalize(work)
    first_in = (unit * norms_full[0] + norms_full[1]).astype(BF)
    second_in = (unit * norms_full[2] + norms_full[3]).astype(BF)
    attend_in = rows_of(attend_mine, attend_other)
    attend_in = attend_in.swapaxes(0, 1).reshape(3, width, inner)
    attended, query, keys, values = attention(first_in, attend_in, tables, half, 0)
    second_in, contract_mine, attended, expand_other = lax.optimization_barrier(
        (second_in, contract_mine, attended, expand_other)
    )
    contract_other = swap(contract_mine)
    expand = rows_of(expand_mine, expand_other).reshape(width, units)
    hidden, slope_units = hidden_units(second_in, expand, half)
    frozen_low, hidden = lax.optimization_barrier((frozen_low, hidden))
    frozen_stats, _, _ = head_stats(frozen_low, vocab_table, targets)
    frozen_peak, frozen_total, frozen_picked = join_stats(frozen_stats)
    hidden, frozen_peak = lax.optimization_barrier((hidden, frozen_peak))

    contract, attend_out = (contract_mine, contract_other), (out_mine, out_other)
    scored_halves = tensor_halves(
        jnp.concatenate(
            [
                branch_terms(hidden, attended, contract, attend_out, g * half, half)
                for g in (1, 2)
            ],
            axis=0,
        )
    )
    unit_out, unit_low, inverse_out, out_low = out_rows(
        jnp.concatenate([policy_rows[half:], other[1]], axis=0), scored_halves
    )
    stats, logits, target_hit = head_stats(unit_low, vocab_table, targets)
    peak, total, picked = join_stats(stats)
    softmax_part = jnp.exp(logits - peak[:, None]) * (1.0 / total)[:, None]
    pull_logits = (target_hit.astype(F32) - softmax_part).astype(BF)

    log_chance = jnp.stack(
        [picked - peak - jnp.log(total), frozen_picked - frozen_peak - jnp.log(frozen_total)]
    )
    steps = jnp.arange(half, dtype=jnp.int32)
    own_count = answer_len[own_index]
    other_count = answer_len[other_index]
    own_live = (steps < own_count).astype(F32)
    other_live = (steps < other_count).astype(F32)
    own_total = own_count.astype(F32)
    other_total = other_count.astype(F32)
    own_mean = jnp.sum(log_chance[:, :half] * own_live, axis=1) / own_total
    other_mean = jnp.sum(log_chance[:, half:] * other_live, axis=1) / other_total
    gaps = jnp.stack([own_mean[0] - own_mean[1], other_mean[0] - other_mean[1]])
    every, back_parts = back_columns(pull_logits, vocab_table, gaps)
    back_parts = [whole_rows(*part) for part in back_parts]
    drift = jnp.sum(every[:, 1]) / groups
    sign = (2 * desirable - 1).astype(F32)
    settled = jax.nn.sigmoid(KTO_BETA * sign * (every[:, 0] - jax.nn.softplus(drift)))
    slope = KTO_BETA * sign * settled * (1.0 - settled)
    loss_total = jnp.sum(1.0 - settled)
    pull = jnp.sum(slope) * jax.nn.sigmoid(drift) / groups
    row_weight = jnp.concatenate(
        [-slope[own_index] * own_live / own_total, pull * other_live / other_total]
    )

    back_unit = row_weight[:, None] * jnp.concatenate(back_parts, axis=1).astype(F32)
    back_out = normalize_back(back_unit, unit_out, inverse_out)
    branch_low = back_out.astype(BF)

    features_scored = jnp.concatenate([hidden[half:], attended[half:]], axis=1)
    near_features, far_features = features_scored[:, :cut][None], features_scored[:, cut:][None]
    near_sent = grad_blocks(branch_low, near_features, (1,))
    near_came = swap(near_sent)
    far_blocks = grad_blocks(branch_low, far_features, range(pair))
    far_back = scatter_ring(far_blocks)

    contract_full = columns_of(*contract)
    back_expand = (dot(branch_low, contract_full, NT) * slope_units).astype(BF)
    expand_sent = grad_blocks(second_in[half:], back_expand[None], (1,))
    expand_came = swap(expand_sent)
    back_attended = dot(branch_low, columns_of(*attend_out), NT).astype(BF)
    back_three = attention_back(back_attended, query, keys, values, tables, half)
    attend_sent = grad_blocks(first_in, back_three, (1,))
    attend_came = swap(attend_sent)

    kept_left = after(branch_low, far_blocks, expand_sent, attend_sent)
    near_ring = to_ring(grad_blocks(kept_left, near_features, (0,)), near_came)
    grad_near = scatter_ring(near_ring)[0].astype(F32)
    second_scored, near_ring, far_back = lax.optimization_barrier(
        (second_in[half:], near_ring, far_back)
    )
    expand_kept = grad_blocks(second_scored, back_expand[None], (0,))
    expand_ring = to_ring(expand_kept, expand_came)
    grad_expand = scatter_ring(expand_ring)[0].astype(F32)
    back_expand, back_three, expand_ring = lax.optimization_barrier(
        (back_expand, back_three, expand_ring)
    )
    back_second = dot(back_expand, expand, NT)
    back_first = sum(dot(back_three[i], attend_in[i], NT) for i in range(3))

    unit_scored = unit[half:]
    grad_norms = sum_small(
        jnp.stack(
            [
                jnp.sum(back_first * unit, axis=0),
                jnp.sum(back_first, axis=0),
                jnp.sum(back_second * unit_scored, axis=0),
                jnp.sum(back_second, axis=0),
            ]
        ),
        ("tensor",),
    )
    back_h = back_first * norms_full[0] + jnp.pad(
        back_second * norms_full[2], ((half, 0), (0, 0))
    )
    back_h, attend_came = lax.optimization_barrier((tensor_sum(back_h), attend_came))
    attend_kept = grad_blocks(after(first_in, back_h), back_three, (0,))
    attend_ring = to_ring(attend_kept, attend_came)
    attend_back = scatter_ring(attend_ring)
    back_work = normalize_back(
        after(back_h, attend_ring).astype(F32), unit, inverse_scale
    ) + jnp.pad(back_out, ((half, 0), (0, 0)))
    out_prompt = work[:half] + tensor_sum(
        branch_terms(hidden, attended, contract, attend_out, 0, half)
    ).astype(F32)
    mixed = jnp.concatenate([out_prompt.astype(BF), out_low[:half]], axis=0)
    grad_norms = sum_small(after(grad_norms, attend_ring), ("dp",))
    grad_norms = lax.dynamic_slice_in_dim(grad_norms, own_index * slab, slab, 1)
    returned = borrow_rows(back_work[None, 2 * half :].astype(BF), inverse, attend_ring)[0]
    grad_far = far_back[0, 0].astype(F32)
    if pair == 2:
        grad_far = grad_far + pair_swap(far_back[1, 0]).astype(F32)
    grad_join = jnp.concatenate([grad_near.T, grad_far.T], axis=0)
    grad_contract, grad_attend_out = grad_join[:units], grad_join[units:]
    input_grad = jnp.concatenate(
        [back_work[:half], back_work[half : 2 * half] + returned.astype(F32)], axis=0
    )

    matrix_rate = 0.5 * D ** (-0.5)
    out_rate = 0.5 * max(D // HALF, 1) ** (-0.5)
    masters = (norms_master, attend_in_master, attend_out_master, expand_master, contract_master)
    firsts = (norms_first, attend_in_first, attend_out_first, expand_first, contract_first)
    seconds = (norms_second, attend_in_second, attend_out_second, expand_second, contract_second)
    rates = (NORM_RATE, matrix_rate, out_rate, matrix_rate, matrix_rate)
    decays = (0.0, DECAY_RATE, DECAY_RATE, DECAY_RATE, DECAY_RATE)
    gradients = [grad_norms, None, grad_attend_out, grad_expand, grad_contract]
    updated = [None] * 5
    for i in (2, 4, 3, 0):
        updated[i] = adamw_step(
            masters[i], firsts[i], seconds[i], gradients[i], rates[i], decays[i]
        )
    attend_back, *waited = lax.optimization_barrier(
        (attend_back, *(updated[i][0] for i in (2, 4, 3, 0)))
    )
    for i, first in zip((2, 4, 3, 0), waited):
        updated[i] = (first,) + updated[i][1:]
    updated[1] = adamw_step(
        masters[1], firsts[1], seconds[1], attend_back.astype(F32), rates[1], decays[1]
    )
    return (
        mixed,
        input_grad,
        jnp.reshape(loss_total, (1,)),
        *(step[0] for step in updated),
        *(step[1] for step in updated),
        *(step[2] for step in updated),
    )


def solution(mesh):
    rows = P("dp", None)
    all_of = P()
    state = (P(None, "dp"), P(None, "dp", "tensor"), P("tensor", "dp"), P("dp", "tensor"), P("tensor", "dp"))
    frozen = (all_of, P(None, None, "tensor"), P("tensor", None), P(None, "tensor"), P("tensor", None))
    return jax.shard_map(
        per_device,
        mesh=mesh,
        in_specs=(rows, rows) + (all_of,) * 4 + state * 4 + frozen + (P(None, "tensor"),),
        out_specs=(rows, rows, all_of) + state * 3,
        check_vma=False,
    )
```

```python
import jax
import jax.numpy as jnp
from jax import lax
from jax.experimental import pallas as pl
from jax.experimental.pallas import tpu as pltpu
from jax.sharding import PartitionSpec as P

D = 2048
HD = 128
ROT = 32
HALF = 256
STEP = 10


NORM_EPSILON = 1e-05
KTO_BETA = 2.0
ADAM_ONE = 0.9
ADAM_TWO = 0.95
ADAM_EPSILON = 1e-08
DECAY_RATE = 0.1
NORM_RATE = 0.3
ROPE_BASE = 10000.0
MASKED = -1e30

LIGHT = pl.CostEstimate(flops=1, bytes_accessed=1, transcendentals=0)
BF = jnp.bfloat16
F32 = jnp.float32


def dot(a, b, dims):
    return lax.dot_general(a, b, (dims, ((), ())), preferred_element_type=F32)


NN = ((1,), (0,))
NT = ((1,), (1,))
TN = ((0,), (0,))


def dp_shape():
    groups = lax.axis_size("dp")
    pair = 2 if groups % 2 == 0 else 1
    return groups, pair, groups // pair


def pair_swap(value):
    groups, _, _ = dp_shape()
    return lax.ppermute(value, "dp", [(i, i ^ 1) for i in range(groups)])


def dp_place():
    _, pair, _ = dp_shape()
    own = lax.axis_index("dp")
    return own // pair, own % pair


def tensor_swap(value, bit):
    return lax.ppermute(value, "tensor", [(i, i ^ bit) for i in range(lax.axis_size("tensor"))])


def ring_groups():
    _, pair, ring = dp_shape()
    return [[r * pair + p for r in range(ring)] for p in range(pair)]


def gather_ring(piece):
    return lax.all_gather(piece, "dp", axis_index_groups=ring_groups())


def scatter_ring(blocks):
    return lax.psum_scatter(blocks, "dp", axis_index_groups=ring_groups())


def by_side(mine, other, axis):
    _, low = dp_place()
    first, second = jnp.stack([mine, other], axis), jnp.stack([other, mine], axis)
    return jnp.where(low == 0, first, second)


def rows_of(mine, other):
    if other is None:
        return mine
    both = by_side(mine, other, 1)
    return both.reshape((-1,) + both.shape[2:])


def to_ring(kept, came):
    if came is not None:
        kept = (kept.astype(F32) + came.astype(F32)).astype(BF)
    return kept[:, 0]


def columns_of(mine, other):
    both = mine[:, None] if other is None else by_side(mine, other, 1)
    ring, pair, rows, slab = both.shape
    return jnp.moveaxis(both, 2, 0).reshape(rows, ring * pair * slab)


def gather_step(held, bit):
    groups = lax.axis_size("dp")
    came = lax.ppermute(held, "dp", [(i, i ^ bit) for i in range(groups)])
    return jnp.where(
        lax.axis_index("dp") & bit == 0,
        jnp.concatenate([held, came]),
        jnp.concatenate([came, held]),
    )


def gather_small(value):
    groups = lax.axis_size("dp")
    if groups & (groups - 1):
        return lax.all_gather(value, "dp")
    held = value[None]
    bit = 1
    while bit < groups:
        held = gather_step(held, bit)
        bit *= 2
    return held


def sum_small(value, axes):
    for axis in axes:
        size = lax.axis_size(axis)
        if size & (size - 1):
            value = lax.psum(value, axis)
            continue
        bit = 1
        while bit < size:
            value = value + lax.ppermute(value, axis, [(i, i ^ bit) for i in range(size)])
            bit *= 2
    return value


def tensor_near(part):
    part = part.astype(BF)
    low = lax.axis_index("tensor") % 2
    half = part.shape[0] // 2
    kept = lax.dynamic_slice_in_dim(part, low * half, half, 0)
    sent = lax.dynamic_slice_in_dim(part, (1 - low) * half, half, 0)
    return (kept.astype(F32) + tensor_swap(sent, 1).astype(F32)).astype(BF)


def tensor_far(kept):
    return (kept.astype(F32) + tensor_swap(kept, 2).astype(F32)).astype(BF)


def tensor_halves(part):
    part = part.astype(BF)
    if lax.axis_size("tensor") != 4:
        whole = lax.psum(part, "tensor")
        half = part.shape[0] // 2
        return whole[:half], whole[half:], jnp.zeros((1,), jnp.int32)
    kept = tensor_far(tensor_near(part))
    return kept, tensor_swap(kept, 1), (lax.axis_index("tensor") % 2).reshape(1)


def whole_rows(mine, other, low):
    return jnp.where(
        low[0] == 0, jnp.concatenate([mine, other], axis=0), jnp.concatenate([other, mine], axis=0)
    )


def tensor_sum(part):
    return whole_rows(*tensor_halves(part))


def tensor_join(part):
    if lax.axis_size("tensor") != 4:
        return lax.all_gather(part, "tensor")
    me = lax.axis_index("tensor")
    far = tensor_swap(part, 2)
    two = jnp.where(me // 2 == 0, jnp.stack([part, far]), jnp.stack([far, part]))
    near = tensor_swap(two, 1)
    four = jnp.where(me % 2 == 0, jnp.stack([two, near], 1), jnp.stack([near, two], 1))
    return four.reshape((4,) + part.shape)


def normalize(values):
    centre = jnp.mean(values, axis=-1, keepdims=True)
    centred = values - centre
    inverse_scale = lax.rsqrt(jnp.mean(centred * centred, axis=-1, keepdims=True) + NORM_EPSILON)
    return (centred * inverse_scale, inverse_scale)


def normalize_back(upstream, unit, inverse_scale):
    return inverse_scale * (
        upstream
        - jnp.mean(upstream, axis=-1, keepdims=True)
        - unit * jnp.mean(upstream * unit, axis=-1, keepdims=True)
    )


def after(value, *others):
    return lax.optimization_barrier((value,) + others)[0]


def turn_tables(half):
    place = jnp.arange(3 * half, dtype=jnp.int32)
    place = jnp.where(place < 2 * half, place, place - half)
    freqs = ROPE_BASE ** (-jnp.arange(ROT // 2, dtype=F32) * 2.0 / ROT)
    angles = place.astype(F32)[:, None] * freqs[None, :]
    cosines, sines = jnp.cos(angles), jnp.sin(angles)
    rest = jnp.zeros((3 * half, HD - ROT), F32)
    none = jnp.zeros_like(sines)
    return jnp.stack(
        [
            jnp.concatenate([cosines, cosines, rest + 1.0], axis=1),
            jnp.concatenate([-sines, none, rest], axis=1),
            jnp.concatenate([none, sines, rest], axis=1),
        ]
    )


def turned(x, table, way):
    step = ROT // 2
    moved = pltpu.roll(x, HD - step, 1) * table[1] + pltpu.roll(x, step, 1) * table[2]
    return x * table[0] + moved * way


def seen_scores(query, near, far, half):
    scale = HD ** (-0.5)
    rows = lax.broadcasted_iota(jnp.int32, (half, half), 0)
    cols = lax.broadcasted_iota(jnp.int32, (half, half), 1)
    own = jnp.where(cols <= rows, dot(query, near, NT) * scale, MASKED)
    peak = jnp.max(own, axis=1, keepdims=True)
    if far is None:
        own = jnp.exp(own - peak)
        return own / jnp.sum(own, axis=1, keepdims=True), None
    before = dot(query, far, NT) * scale
    peak = jnp.maximum(peak, jnp.max(before, axis=1, keepdims=True))
    own, before = jnp.exp(own - peak), jnp.exp(before - peak)
    total = jnp.sum(own, axis=1, keepdims=True) + jnp.sum(before, axis=1, keepdims=True)
    return own / total, before / total


def attend_body(half, skip, x_ref, w_ref, t_ref, out_ref, q_ref, k_ref, v_ref):
    x = x_ref[...]
    raw = [dot(x[skip:], w_ref[0], NN), dot(x, w_ref[1], NN), dot(x, w_ref[2], NN)]
    for h in range(w_ref.shape[2] // HD):
        at = slice(h * HD, (h + 1) * HD)
        query = turned(raw[0][:, at], t_ref[:, skip:], 1.0).astype(BF)
        keys = turned(raw[1][:, at], t_ref[...], 1.0).astype(BF)
        values = raw[2][:, at].astype(BF)
        q_ref[:, at], k_ref[:, at], v_ref[:, at] = query, keys, values
        part = lambda x, g, gone=0: x[g * half - gone : (g + 1) * half - gone]
        for g in range(skip // half, 3):
            own, before = seen_scores(
                part(query, g, skip), part(keys, g), part(keys, 0) if g else None, half
            )
            seen = dot(own.astype(BF), part(values, g), NN)
            if g:
                seen = seen + dot(before.astype(BF), part(values, 0), NN)
            out_ref[g * half - skip : (g + 1) * half - skip, at] = seen.astype(BF)


def head_pairs(inner):
    return 2 * HD if inner % (2 * HD) == 0 else HD


def attention(first_in, weights, tables, half, skip):
    count, width = first_in.shape
    inner = weights.shape[2]
    block = head_pairs(inner)
    columns = lambda rows: pl.BlockSpec((rows, block), lambda h: (0, h))
    shape = lambda rows: jax.ShapeDtypeStruct((rows, inner), BF)
    return pl.pallas_call(
        lambda *refs: attend_body(half, skip, *refs),
        grid=(inner // block,),
        in_specs=[
            pl.BlockSpec((count, width), lambda h: (0, 0)),
            pl.BlockSpec((3, width, block), lambda h: (0, 0, h)),
            pl.BlockSpec(tables.shape, lambda h: (0, 0, 0)),
        ],
        out_specs=[columns(count - skip), columns(count - skip), columns(count), columns(count)],
        out_shape=[shape(count - skip), shape(count - skip), shape(count), shape(count)],
        compiler_params=pltpu.CompilerParams(vmem_limit_bytes=48 * 2**20),
        cost_estimate=LIGHT,
        name="attend",
    )(first_in, weights, tables)


def attend_back_body(half, d_ref, q_ref, k_ref, v_ref, t_ref, out_ref):
    scale = HD ** (-0.5)
    for h in range(d_ref.shape[1] // HD):
        at = slice(h * HD, (h + 1) * HD)
        part = lambda ref, g: ref[g * half : (g + 1) * half, at]
        back_keys = back_values = None
        for g in (1, 2):
            query, far, near = part(q_ref, g), part(k_ref, 0), part(k_ref, g)
            upstream = part(d_ref, g - 1)
            own, before = seen_scores(query, near, far, half)
            own_pull = dot(upstream, part(v_ref, g), NT)
            far_pull = dot(upstream, part(v_ref, 0), NT)
            mean = jnp.sum(own * own_pull, axis=1, keepdims=True) + jnp.sum(
                before * far_pull, axis=1, keepdims=True
            )
            own_back = (own * (own_pull - mean)).astype(BF)
            far_back = (before * (far_pull - mean)).astype(BF)
            back_query = (dot(own_back, near, NN) + dot(far_back, far, NN)) * scale
            rows = slice(g * half, (g + 1) * half)
            out_ref[0, rows, at] = turned(
                back_query, t_ref[:, rows], -1.0
            ).astype(BF)
            out_ref[1, rows, at] = turned(
                dot(own_back, query, TN) * scale, t_ref[:, rows], -1.0
            ).astype(BF)
            out_ref[2, rows, at] = dot(own.astype(BF), upstream, TN).astype(BF)
            more_keys, more_values = dot(far_back, query, TN), dot(before.astype(BF), upstream, TN)
            back_keys = more_keys if back_keys is None else back_keys + more_keys
            back_values = more_values if back_values is None else back_values + more_values
        out_ref[0, :half, at] = jnp.zeros((half, HD), BF)
        out_ref[1, :half, at] = turned(back_keys * scale, t_ref[:, :half], -1.0).astype(BF)
        out_ref[2, :half, at] = back_values.astype(BF)


def attention_back(back_attended, query, keys, values, tables, half):
    count, inner = keys.shape
    block = head_pairs(inner)
    columns = lambda rows: pl.BlockSpec((rows, block), lambda h: (0, h))
    return pl.pallas_call(
        lambda *refs: attend_back_body(half, *refs),
        grid=(inner // block,),
        in_specs=[
            columns(count - half),
            columns(count),
            columns(count),
            columns(count),
            pl.BlockSpec(tables.shape, lambda h: (0, 0, 0)),
        ],
        out_specs=pl.BlockSpec((3, count, block), lambda h: (0, 0, h)),
        out_shape=jax.ShapeDtypeStruct((3, count, inner), BF),
        compiler_params=pltpu.CompilerParams(vmem_limit_bytes=48 * 2**20),
        cost_estimate=LIGHT,
        name="attend_back",
    )(back_attended, query, keys, values, tables)


def hidden_body(skip, before, out_ref, *slope_ref):
    share = 0.5 + 0.5 * lax.erf(before * 0.5**0.5)
    out_ref[...] = (before * share).astype(BF)
    if slope_ref:
        kept = before[skip:]
        bell = jnp.exp(-0.5 * kept * kept) * (2.0 * jnp.pi) ** (-0.5)
        slope_ref[0][...] = share[skip:] + kept * bell


def over_shards(pair, low_ref, x_ref, w_refs, rows_first):
    total = None
    ring = w_refs[0].shape[0]
    slab = w_refs[0].shape[1 if rows_first else 2]
    for side in range(pair):
        for r in range(ring):
            at = pl.multiple_of(shard_of(r, side, low_ref, pair) * slab, slab)
            term = dot(x_ref[:, pl.ds(at, slab)], w_refs[side][r], NN if rows_first else NT)
            total = term if total is None else total + term
    return total


def hidden_units(second_in, expand, skip=None):
    count, width = second_in.shape
    pair = dp_shape()[1]
    if isinstance(expand, tuple) and expand[0].shape[1] % 128:
        expand = rows_of(*expand).reshape(width, -1)
    sides = isinstance(expand, tuple)
    units = expand[0].shape[2] if sides else expand.shape[1]
    block = 256
    column = lambda rows: pl.BlockSpec((rows, block), lambda i, l: (0, i))
    weights = list(expand[:pair]) if sides else [expand]
    weight_specs = [
        pl.BlockSpec(x.shape[:2] + (block,), lambda i, l: (0, 0, i)) if sides else column(width)
        for x in weights
    ]
    out_specs, out_shape = [column(count)], [jax.ShapeDtypeStruct((count, units), BF)]
    if skip is not None:
        out_specs.append(column(count - skip))
        out_shape.append(jax.ShapeDtypeStruct((count - skip, units), F32))

    def body(low_ref, x_ref, *refs):
        w_refs, out_refs = refs[: len(weights)], refs[len(weights) :]
        if sides:
            before = over_shards(pair, low_ref, x_ref, w_refs, True)
        else:
            before = dot(x_ref[...], w_refs[0][...], NN)
        hidden_body(skip, before, *out_refs)

    return pl.pallas_call(
        body,
        grid_spec=pltpu.PrefetchScalarGridSpec(
            num_scalar_prefetch=1,
            grid=(units // block,),
            in_specs=[pl.BlockSpec((count, width), lambda i, l: (0, 0)), *weight_specs],
            out_specs=out_specs,
        ),
        out_shape=out_shape,
        compiler_params=pltpu.CompilerParams(vmem_limit_bytes=48 * 2**20),
        cost_estimate=LIGHT,
        name="hidden",
    )(dp_place()[1].reshape(1), second_in, *weights)


def pull_units(branch_low, weights, slope=None):
    rows, width = branch_low.shape
    pair = dp_shape()[1]
    units, slab = weights[0].shape[1:]
    if slab % 128:
        out = dot(branch_low, columns_of(*weights), NT)
        return (out if slope is None else out * slope).astype(BF)
    block = 256
    weights = list(weights[:pair])
    column = pl.BlockSpec((rows, block), lambda i, l: (0, i))

    def body(low_ref, x_ref, *refs):
        out = over_shards(pair, low_ref, x_ref, refs[:pair], False)
        if slope is not None:
            out = out * refs[pair][...]
        refs[-1][...] = out.astype(BF)

    return pl.pallas_call(
        body,
        grid_spec=pltpu.PrefetchScalarGridSpec(
            num_scalar_prefetch=1,
            grid=(units // block,),
            in_specs=[
                pl.BlockSpec((rows, width), lambda i, l: (0, 0)),
                *(
                    pl.BlockSpec((x.shape[0], block, slab), lambda i, l: (0, i, 0))
                    for x in weights
                ),
                *([] if slope is None else [column]),
            ],
            out_specs=column,
        ),
        out_shape=jax.ShapeDtypeStruct((rows, units), BF),
        compiler_params=pltpu.CompilerParams(vmem_limit_bytes=48 * 2**20),
        cost_estimate=LIGHT,
        name="pull_units",
    )(dp_place()[1].reshape(1), branch_low, *weights, *([] if slope is None else [slope]))


def shard_of(r, side, low, pair):
    return r * pair + (low[0] + side) % pair


def grad_body(x_ref, y_ref, out_ref):
    x = x_ref[...]
    for i in range(y_ref.shape[0]):
        out_ref[0, 0, i] = dot(x, y_ref[i], TN).astype(BF)


def grad_blocks(left, right, sides):
    groups, pair, ring = dp_shape()
    low = dp_place()[1].reshape(1)
    rows = left.shape[0]
    slab = left.shape[1] // groups
    parts, _, width = right.shape
    if slab % 128:
        shards = left.reshape(rows, ring, pair, slab)
        shards = jnp.stack([shards[:, :, (low[0] + s) % pair] for s in sides], axis=2)
        out = jnp.einsum("nrsc,pnw->rspcw", shards, right, preferred_element_type=F32)
        return out.astype(BF)
    first = sides[0]
    return pl.pallas_call(
        lambda low_ref, *refs: grad_body(*refs),
        grid_spec=pltpu.PrefetchScalarGridSpec(
            num_scalar_prefetch=1,
            grid=(ring, len(sides)),
            in_specs=[
                pl.BlockSpec((rows, slab), lambda r, s, l: (0, shard_of(r, s + first, l, pair))),
                pl.BlockSpec(right.shape, lambda r, s, l: (0, 0, 0)),
            ],
            out_specs=pl.BlockSpec(
                (1, 1, parts, slab, width), lambda r, s, l: (r, s, 0, 0, 0)
            ),
        ),
        out_shape=jax.ShapeDtypeStruct((ring, len(sides), parts, slab, width), BF),
        compiler_params=pltpu.CompilerParams(vmem_limit_bytes=48 * 2**20),
        cost_estimate=LIGHT,
        name="grad_blocks",
    )(low, left, right)


def branch_terms(hidden, attended, contract, attend_out, blocks, half):
    groups, pair, ring = dp_shape()
    low = dp_place()[1].reshape(1)
    slab = contract[0].shape[2]
    count = half * len(blocks)
    if slab % 128:
        rows = slice(blocks[0] * half, blocks[0] * half + count)
        out = 0.0
        for x, sides in ((hidden[rows], contract), (attended[rows], attend_out)):
            if pair == 2:
                sides = [by_side(sides[0], sides[1], 1)]
            weight = sides[0].reshape(groups, x.shape[1], slab)
            out = out + jnp.einsum("nf,sfc->nsc", x, weight, preferred_element_type=F32)
        return out.reshape(count, groups * slab).astype(BF)
    weights = [*contract[:pair], *attend_out[:pair]]
    row_block = lambda x, b: pl.BlockSpec((half, x.shape[1]), lambda r, s, l: (b, 0))

    def body(low_ref, *refs):
        x_refs, refs = refs[: 2 * len(blocks)], refs[2 * len(blocks) :]

        def write(side):
            for i in range(len(blocks)):
                refs[-1][i * half : (i + 1) * half] = (
                    dot(x_refs[2 * i][...], refs[side][0], NN)
                    + dot(x_refs[2 * i + 1][...], refs[pair + side][0], NN)
                ).astype(BF)

        for side in range(pair):
            pl.when(pl.program_id(1) == side)(lambda: write(side))

    return pl.pallas_call(
        body,
        grid_spec=pltpu.PrefetchScalarGridSpec(
            num_scalar_prefetch=1,
            grid=(ring, pair),
            in_specs=[
                *(row_block(x, b) for b in blocks for x in (hidden, attended)),
                *(pl.BlockSpec((1,) + x.shape[1:], lambda r, s, l: (r, 0, 0)) for x in weights),
            ],
            out_specs=pl.BlockSpec(
                (count, slab), lambda r, s, l: (0, shard_of(r, s, l, pair))
            ),
        ),
        out_shape=jax.ShapeDtypeStruct((count, groups * slab), BF),
        compiler_params=pltpu.CompilerParams(vmem_limit_bytes=48 * 2**20),
        cost_estimate=LIGHT,
        name="branch",
    )(low, *[hidden, attended] * len(blocks), *weights)


def shard_terms(lefts, weights):
    groups, pair, ring = dp_shape()
    low = dp_place()[1].reshape(1)
    weights = list(weights[:pair])
    count = lefts.shape[1]
    parts, slab, depth = weights[0].shape[1:]
    if slab % 128:
        whole = by_side(weights[0], weights[1], 1) if pair == 2 else weights[0]
        whole = whole.reshape(groups, parts, slab, depth)
        out = jnp.einsum("pnk,gpsk->ngs", lefts, whole, preferred_element_type=F32)
        return out.reshape(count, groups * slab)

    def body(low_ref, x_ref, *refs):
        def write(side):
            total = dot(x_ref[0], refs[side][0, 0], NT)
            for i in range(1, parts):
                total = total + dot(x_ref[i], refs[side][0, i], NT)
            refs[-1][...] = total

        for side in range(pair):
            pl.when(pl.program_id(1) == side)(lambda: write(side))

    return pl.pallas_call(
        body,
        grid_spec=pltpu.PrefetchScalarGridSpec(
            num_scalar_prefetch=1,
            grid=(ring, pair),
            in_specs=[
                pl.BlockSpec(lefts.shape, lambda r, s, l: (0, 0, 0)),
                *(pl.BlockSpec((1,) + x.shape[1:], lambda r, s, l: (r, 0, 0, 0)) for x in weights),
            ],
            out_specs=pl.BlockSpec(
                (count, slab), lambda r, s, l: (0, shard_of(r, s, l, pair))
            ),
        ),
        out_shape=jax.ShapeDtypeStruct((count, groups * slab), F32),
        compiler_params=pltpu.CompilerParams(vmem_limit_bytes=48 * 2**20),
        cost_estimate=LIGHT,
        name="shard_terms",
    )(low, lefts, *weights)


def out_body(x_ref, mine_ref, other_ref, low_ref, unit_ref, low_unit_ref, scale_ref, out_ref):
    mine = pl.program_id(0) == low_ref[0]
    branch = jnp.where(mine, mine_ref[...].astype(F32), other_ref[...].astype(F32))
    out = x_ref[...].astype(F32) + branch
    unit, scale = normalize(out)
    unit_ref[...] = unit
    low_unit_ref[...] = unit.astype(BF)
    scale_ref[...] = scale
    out_ref[...] = out.astype(BF)


def out_rows(x, halves):
    mine, other, low = halves
    rows, width = x.shape
    block = 128
    steps = rows // 2 // block
    whole = pl.BlockSpec((block, width), lambda h, i: (h * steps + i, 0))
    part = pl.BlockSpec((block, width), lambda h, i: (i, 0))
    return pl.pallas_call(
        out_body,
        grid=(2, steps),
        in_specs=[whole, part, part, pl.BlockSpec(memory_space=pltpu.SMEM)],
        out_specs=[whole, whole, pl.BlockSpec((block, 1), lambda h, i: (h * steps + i, 0)), whole],
        out_shape=[
            jax.ShapeDtypeStruct((rows, width), F32),
            jax.ShapeDtypeStruct((rows, width), BF),
            jax.ShapeDtypeStruct((rows, 1), F32),
            jax.ShapeDtypeStruct((rows, width), BF),
        ],
        compiler_params=pltpu.CompilerParams(vmem_limit_bytes=48 * 2**20),
        cost_estimate=LIGHT,
        name="out_rows",
    )(x, mine, other, low)


def borrow_rows(tail, order, first=(), last=()):
    groups = lax.axis_size("dp")
    parts = lax.axis_size("tensor")
    count, rows, width = tail.shape
    share = rows // parts
    mine = lax.dynamic_slice_in_dim(tail, lax.axis_index("tensor") * share, share, 1)
    mine = mine.reshape(count, groups, share // groups, width).swapaxes(0, 1)
    spread = after(lax.all_to_all(mine, "dp", split_axis=0, concat_axis=0, tiled=True), *first)
    landed = lax.all_to_all(
        jnp.take(spread, order, axis=0), "dp", split_axis=0, concat_axis=0, tiled=True
    )
    landed = landed.swapaxes(0, 1).reshape(count, share, width)
    return tensor_join(after(landed, *last)).swapaxes(0, 1).reshape(count, rows, width)


TILE = 1280
CHUNK = 256


def head_body(vocab, x_ref, w_ref, t_ref, *refs):
    logits_ref, stats_ref, peak_ref, total_ref, picked_ref = refs if len(refs) == 5 else (None, *refs)
    step = pl.program_id(0)

    @pl.when(step == 0)
    def _():
        peak_ref[...] = jnp.full(peak_ref.shape, MASKED, F32)
        total_ref[...] = jnp.zeros(total_ref.shape, F32)
        picked_ref[...] = jnp.zeros(picked_ref.shape, F32)

    x, target = x_ref[...], t_ref[...]
    lanes = lax.broadcasted_iota(jnp.int32, (x.shape[0], 128), 1)
    for c in range(0, TILE, CHUNK):
        logits = dot(x, w_ref[c : c + CHUNK], NT)
        if logits_ref is not None:
            logits_ref[:, c : c + CHUNK] = logits
        parts = []
        picked = picked_ref[...]
        for d in range(0, CHUNK, 128):
            column = lanes + (step * TILE + c + d)
            part = jnp.where(column < vocab, logits[:, d : d + 128], MASKED)
            picked = picked + jnp.where(column == target, part, 0.0)
            parts.append(part)
        picked_ref[...] = picked
        old = peak_ref[...]
        peak = old
        for part in parts:
            peak = jnp.maximum(peak, part)
        total = total_ref[...] * jnp.exp(old - peak)
        for part in parts:
            total = total + jnp.exp(part - peak)
        peak_ref[...] = peak
        total_ref[...] = total

    @pl.when(step == pl.num_programs(0) - 1)
    def _():
        peak = jnp.max(peak_ref[...], axis=1, keepdims=True)
        total = jnp.sum(total_ref[...] * jnp.exp(peak_ref[...] - peak), axis=1, keepdims=True)
        picked = jnp.sum(picked_ref[...], axis=1, keepdims=True)
        rows = jnp.where(lanes == 0, peak, jnp.where(lanes == 1, total, picked))
        stats_ref[...] = rows.T[:8]


def head_stats(unit_low, table, local_targets, keep):
    rows, width = unit_low.shape
    vocab = table.shape[0]
    tiles = pl.cdiv(vocab, TILE)
    out_specs = [pl.BlockSpec((8, rows), lambda i: (0, 0))]
    out_shape = [jax.ShapeDtypeStruct((8, rows), F32)]
    if keep:
        out_specs.insert(0, pl.BlockSpec((rows, TILE), lambda i: (0, i)))
        out_shape.insert(0, jax.ShapeDtypeStruct((rows, vocab), F32))
    out = pl.pallas_call(
        lambda *refs: head_body(vocab, *refs),
        grid=(tiles,),
        in_specs=[
            pl.BlockSpec((rows, width), lambda i: (0, 0)),
            pl.BlockSpec((TILE, width), lambda i: (i, 0)),
            pl.BlockSpec((rows, 1), lambda i: (0, 0)),
        ],
        out_specs=out_specs,
        out_shape=out_shape,
        scratch_shapes=[pltpu.VMEM((rows, 128), F32)] * 3,
        compiler_params=pltpu.CompilerParams(vmem_limit_bytes=48 * 2**20),
        cost_estimate=LIGHT,
        name="head",
    )(unit_low, table, local_targets[:, None])
    return out[-1][:3], out[0] if keep else None


def head_pull_body(vocab, tiles, x_ref, w_ref, row_ref, t_ref, out_ref, pull_ref, total_ref):
    step = pl.program_id(0)

    @pl.when(step == 0)
    def _():
        total_ref[...] = jnp.zeros(total_ref.shape, F32)

    def add(masked):
        for c in range(0, TILE, CHUNK):
            at = slice(c, c + CHUNK)
            column = lax.broadcasted_iota(jnp.int32, (x_ref.shape[0], CHUNK), 1)
            column = column + (step * TILE + c)
            pull = jnp.where(column == t_ref[...], 1.0, 0.0) - jnp.exp(
                x_ref[:, at] - row_ref[:, 0:1]
            ) * row_ref[:, 1:2]
            if masked:
                pull = jnp.where(column < vocab, pull, 0.0)
            pull_ref[:, at] = pull.astype(BF)
        width = w_ref.shape[1]
        for c in range(0, width, width // 4):
            at = slice(c, c + width // 4)
            weight = w_ref[:, at]
            if masked:
                seen = lax.broadcasted_iota(jnp.int32, weight.shape, 0)
                seen = seen < vocab - (tiles - 1) * TILE
                weight = jnp.where(seen, weight.astype(F32), 0.0).astype(BF)
            total_ref[:, at] += dot(pull_ref[...], weight, NN)

    pl.when(step < tiles - 1)(lambda: add(False))
    pl.when(step == tiles - 1)(lambda: add(True))

    @pl.when(step == tiles - 1)
    def _():
        out_ref[...] = total_ref[...].astype(BF)


def head_pull(logits, table, row, targets):
    rows, vocab = logits.shape
    width = table.shape[1]
    tiles = pl.cdiv(vocab, TILE)
    whole = lambda x: pl.BlockSpec(x, lambda i: (0, 0))
    return pl.pallas_call(
        lambda *refs: head_pull_body(vocab, tiles, *refs),
        grid=(tiles,),
        in_specs=[
            pl.BlockSpec((rows, TILE), lambda i: (0, i)),
            pl.BlockSpec((TILE, width), lambda i: (i, 0)),
            whole((rows, 2)),
            whole((rows, 1)),
        ],
        out_specs=whole((rows, width)),
        out_shape=jax.ShapeDtypeStruct((rows, width), BF),
        scratch_shapes=[pltpu.VMEM((rows, TILE), BF), pltpu.VMEM((rows, width), F32)],
        compiler_params=pltpu.CompilerParams(vmem_limit_bytes=48 * 2**20),
        cost_estimate=LIGHT,
        name="head_pull",
    )(logits, table, row, targets[:, None])


def join_stats(stats):
    every = lax.all_gather(stats, "tensor")
    peak = jnp.max(every[:, 0], axis=0)
    total = jnp.sum(every[:, 1] * jnp.exp(every[:, 0] - peak[None]), axis=0)
    return peak, total, jnp.sum(every[:, 2], axis=0)


def adamw_step(master, first, second, gradient, rate, decay):
    new_first = ADAM_ONE * first + (1.0 - ADAM_ONE) * gradient
    new_second = ADAM_TWO * second + (1.0 - ADAM_TWO) * gradient * gradient
    ratio = (
        new_first
        / (1.0 - ADAM_ONE**STEP)
        / (jnp.sqrt(new_second / (1.0 - ADAM_TWO**STEP)) + ADAM_EPSILON)
    )
    return (master - rate * (ratio + decay * master), new_first, new_second)


def per_device(
    policy_rows,
    frozen_rows,
    next_tokens,
    desirable,
    answer_len,
    partner,
    norms_copy,
    attend_in_copy,
    attend_out_copy,
    expand_copy,
    contract_copy,
    norms_master,
    attend_in_master,
    attend_out_master,
    expand_master,
    contract_master,
    norms_first,
    attend_in_first,
    attend_out_first,
    expand_first,
    contract_first,
    norms_second,
    attend_in_second,
    attend_out_second,
    expand_second,
    contract_second,
    frozen_norms,
    frozen_in,
    frozen_out,
    frozen_expand,
    frozen_contract,
    vocab_table,
):
    groups = lax.axis_size("dp")
    own_index = lax.axis_index("dp")
    half = policy_rows.shape[0] // 2
    inner = attend_in_copy.shape[2]
    slab = attend_in_copy.shape[1]
    width = policy_rows.shape[1]
    inverse = jnp.zeros_like(partner).at[partner].set(jnp.arange(groups, dtype=jnp.int32))
    other_index = partner[own_index]

    norms_full = gather_small(norms_copy).swapaxes(0, 1).reshape(4, width).astype(F32)
    units = expand_copy.shape[1]
    _, pair, ring = dp_shape()
    _, low = dp_place()
    swap = pair_swap if pair == 2 else (lambda value: None)
    cut = (units + inner) // 2
    out_came = swap(attend_out_copy)
    attend_mine = gather_ring(attend_in_copy)
    expand_mine = gather_ring(expand_copy)
    contract_mine = gather_ring(contract_copy)
    out_mine = gather_ring(attend_out_copy)
    out_other = None if out_came is None else gather_ring(out_came)
    norms_full = norms_full if out_came is None else after(norms_full, out_came)

    other = borrow_rows(jnp.stack([frozen_rows[half:], policy_rows[half:]]), partner)
    other, attend_mine = lax.optimization_barrier((other, attend_mine))
    tables = turn_tables(half)

    frozen_work = jnp.concatenate([frozen_rows, other[0]], axis=0).astype(F32)
    frozen_unit, _ = normalize(frozen_work)
    frozen_first_in = (frozen_unit * frozen_norms[0] + frozen_norms[1]).astype(BF)
    frozen_second_in = (frozen_unit[half:] * frozen_norms[2] + frozen_norms[3]).astype(BF)
    frozen_first_in, frozen_second_in, norms_full = lax.optimization_barrier(
        (frozen_first_in, frozen_second_in, norms_full)
    )
    attend_other = swap(attend_mine)
    frozen_attended = attention(frozen_first_in, frozen_in, tables, half, half)[0]
    (frozen_hidden,) = hidden_units(frozen_second_in, frozen_expand)
    frozen_part = dot(frozen_attended, frozen_out, NN) + dot(frozen_hidden, frozen_contract, NN)
    frozen_part, attend_other, expand_mine = lax.optimization_barrier(
        (frozen_part.astype(BF), attend_other, expand_mine)
    )
    expand_other = swap(expand_mine)
    frozen_low = out_rows(
        jnp.concatenate([frozen_rows[half:], other[0]], axis=0), tensor_halves(frozen_part)
    )[1]
    vocab_local = vocab_table.shape[1]
    table = vocab_table.T
    targets = (
        jnp.concatenate([next_tokens[own_index], next_tokens[other_index]])
        - lax.axis_index("tensor") * vocab_local
    )
    targets = jnp.where((targets >= 0) & (targets < vocab_local), targets, -1)
    work = jnp.concatenate([policy_rows, other[1]], axis=0).astype(F32)
    unit, inverse_scale = normalize(work)
    first_in = (unit * norms_full[0] + norms_full[1]).astype(BF)
    second_in = (unit * norms_full[2] + norms_full[3]).astype(BF)
    attend_in = rows_of(attend_mine, attend_other)
    attend_in = attend_in.swapaxes(0, 1).reshape(3, width, inner)
    attended, query, keys, values = attention(first_in, attend_in, tables, half, 0)
    second_in, contract_mine, attended, expand_other = lax.optimization_barrier(
        (second_in, contract_mine, attended, expand_other)
    )
    contract_other = swap(contract_mine)
    frozen_low, second_in = lax.optimization_barrier((frozen_low, second_in))
    frozen_stats, _ = head_stats(frozen_low, table, targets, False)
    frozen_peak, frozen_total, frozen_picked = join_stats(frozen_stats)
    second_in, frozen_peak = lax.optimization_barrier((second_in, frozen_peak))
    hidden, slope_units = hidden_units(second_in, (expand_mine, expand_other), half)

    contract, attend_out = (contract_mine, contract_other), (out_mine, out_other)
    scored_halves = tensor_halves(
        branch_terms(hidden, attended, contract, attend_out, (1, 2), half)
    )
    unit_out, unit_low, inverse_out, out_low = out_rows(
        jnp.concatenate([policy_rows[half:], other[1]], axis=0), scored_halves
    )
    stats, logits = head_stats(unit_low, table, targets, True)
    peak, total, picked = join_stats(stats)
    log_chance = jnp.stack(
        [picked - peak - jnp.log(total), frozen_picked - frozen_peak - jnp.log(frozen_total)]
    )
    steps = jnp.arange(half, dtype=jnp.int32)
    own_count = answer_len[own_index]
    other_count = answer_len[other_index]
    own_live = (steps < own_count).astype(F32)
    other_live = (steps < other_count).astype(F32)
    own_total = own_count.astype(F32)
    other_total = other_count.astype(F32)
    own_mean = jnp.sum(log_chance[:, :half] * own_live, axis=1) / own_total
    other_mean = jnp.sum(log_chance[:, half:] * other_live, axis=1) / other_total
    gaps = jnp.stack([own_mean[0] - own_mean[1], other_mean[0] - other_mean[1]])
    row = jnp.stack([peak, 1.0 / total], axis=1)
    every = gather_small(gaps)
    back_part = head_pull(logits, table, row, targets)
    back_sum = tensor_sum(back_part)
    drift = jnp.sum(every[:, 1]) / groups
    sign = (2 * desirable - 1).astype(F32)
    settled = jax.nn.sigmoid(KTO_BETA * sign * (every[:, 0] - jax.nn.softplus(drift)))
    slope = KTO_BETA * sign * settled * (1.0 - settled)
    loss_total = jnp.sum(1.0 - settled)
    pull = jnp.sum(slope) * jax.nn.sigmoid(drift) / groups
    row_weight = jnp.concatenate(
        [-slope[own_index] * own_live / own_total, pull * other_live / other_total]
    )

    back_unit = row_weight[:, None] * back_sum.astype(F32)
    back_out = normalize_back(back_unit, unit_out, inverse_out)
    branch_low = back_out.astype(BF)

    features_scored = jnp.concatenate([hidden[half:], attended[half:]], axis=1)
    near_features, far_features = features_scored[:, :cut][None], features_scored[:, cut:][None]
    near_sent = grad_blocks(branch_low, near_features, (1,))
    near_came = swap(near_sent)
    branch_low = after(branch_low, near_sent)
    far_blocks = grad_blocks(branch_low, far_features, range(pair))
    far_back = scatter_ring(far_blocks)

    branch_low = after(branch_low, far_blocks)
    back_expand = pull_units(branch_low, contract, slope_units)
    expand_sent = grad_blocks(second_in[half:], back_expand[None], (1,))
    near_kept = grad_blocks(after(branch_low, expand_sent), near_features, (0,))
    near_ring = to_ring(near_kept, near_came)
    grad_near = scatter_ring(near_ring)[0].astype(F32)

    expand_sent, branch_low, back_expand, near_ring = lax.optimization_barrier(
        (expand_sent, branch_low, back_expand, near_ring)
    )
    expand_came = swap(expand_sent)
    back_attended = pull_units(branch_low, attend_out)
    back_three = attention_back(back_attended, query, keys, values, tables, half)
    attend_sent = grad_blocks(first_in, back_three, (1,))
    second_scored, far_back = lax.optimization_barrier((second_in[half:], far_back, attend_sent))[:2]
    expand_kept = grad_blocks(second_scored, back_expand[None], (0,))
    expand_ring = to_ring(expand_kept, expand_came)
    expand_back = scatter_ring(expand_ring)

    attend_sent, back_expand, back_three, expand_ring = lax.optimization_barrier(
        (attend_sent, back_expand, back_three, expand_ring)
    )
    attend_came = swap(attend_sent)
    sided = lambda sides: [x if x is None else x[:, None] for x in sides]
    back_second = shard_terms(back_expand[None], sided((expand_mine, expand_other)))
    back_first = shard_terms(back_three, (attend_mine, attend_other))

    unit_scored = unit[half:]
    grad_norms = sum_small(
        jnp.stack(
            [
                jnp.sum(back_first * unit, axis=0),
                jnp.sum(back_first, axis=0),
                jnp.sum(back_second * unit_scored, axis=0),
                jnp.sum(back_second, axis=0),
            ]
        ),
        ("tensor",),
    )
    back_h = back_first * norms_full[0] + jnp.pad(
        back_second * norms_full[2], ((half, 0), (0, 0))
    )
    four = lax.axis_size("tensor") == 4
    back_h = tensor_near(back_h) if four else lax.psum(back_h.astype(BF), "tensor")
    attend_kept = grad_blocks(after(first_in, back_h), back_three, (0,))
    attend_ring = to_ring(attend_kept, attend_came)
    across = tensor_swap(back_h, 2) if four else back_h
    attend_ring, expand_back, across = lax.optimization_barrier((attend_ring, expand_back, across))
    if four:
        back_h = (back_h.astype(F32) + across.astype(F32)).astype(BF)
        low_row = (lax.axis_index("tensor") % 2).reshape(1)
        back_h = whole_rows(back_h, tensor_swap(back_h, 1), low_row)
    grad_expand = expand_back[0].astype(F32)
    attend_back = scatter_ring(attend_ring)
    hidden = after(hidden, attend_ring)
    back_work = normalize_back(
        back_h.astype(F32), unit, inverse_scale
    ) + jnp.pad(back_out, ((half, 0), (0, 0)))
    out_prompt = work[:half] + tensor_sum(
        branch_terms(hidden, attended, contract, attend_out, (0,), half)
    ).astype(F32)
    mixed = jnp.concatenate([out_prompt.astype(BF), out_low[:half]], axis=0)
    grad_norms = sum_small(after(grad_norms, attend_ring), ("dp",))
    grad_norms = lax.dynamic_slice_in_dim(grad_norms, own_index * slab, slab, 1)
    returned = borrow_rows(back_work[None, 2 * half :].astype(BF), inverse, (attend_ring,), (attend_back,))[0]
    grad_far = far_back[0, 0].astype(F32)
    if pair == 2:
        grad_far = grad_far + pair_swap(after(far_back[1, 0], attend_ring)).astype(F32)
    grad_join = jnp.concatenate([grad_near.T, grad_far.T], axis=0)
    grad_contract, grad_attend_out = grad_join[:units], grad_join[units:]
    input_grad = jnp.concatenate(
        [back_work[:half], back_work[half : 2 * half] + returned.astype(F32)], axis=0
    )

    matrix_rate = 0.5 * D ** (-0.5)
    out_rate = 0.5 * max(D // HALF, 1) ** (-0.5)
    masters = (norms_master, attend_in_master, attend_out_master, expand_master, contract_master)
    firsts = (norms_first, attend_in_first, attend_out_first, expand_first, contract_first)
    seconds = (norms_second, attend_in_second, attend_out_second, expand_second, contract_second)
    rates = (NORM_RATE, matrix_rate, out_rate, matrix_rate, matrix_rate)
    decays = (0.0, DECAY_RATE, DECAY_RATE, DECAY_RATE, DECAY_RATE)
    gradients = [grad_norms, None, grad_attend_out, grad_expand, grad_contract]
    updated = [None] * 5
    for i in (2, 4, 3, 0):
        updated[i] = adamw_step(
            masters[i], firsts[i], seconds[i], gradients[i], rates[i], decays[i]
        )
    attend_back, *waited = lax.optimization_barrier(
        (attend_back, *(updated[i][0] for i in (2, 4, 3, 0)))
    )
    for i, first in zip((2, 4, 3, 0), waited):
        updated[i] = (first,) + updated[i][1:]
    updated[1] = adamw_step(
        masters[1], firsts[1], seconds[1], attend_back.astype(F32), rates[1], decays[1]
    )
    return (
        mixed,
        input_grad,
        jnp.reshape(loss_total, (1,)),
        *(step[0] for step in updated),
        *(step[1] for step in updated),
        *(step[2] for step in updated),
    )


def solution(mesh):
    rows = P("dp", None)
    all_of = P()
    state = (P(None, "dp"), P(None, "dp", "tensor"), P("tensor", "dp"), P("dp", "tensor"), P("tensor", "dp"))
    frozen = (all_of, P(None, None, "tensor"), P("tensor", None), P(None, "tensor"), P("tensor", None))
    return jax.shard_map(
        per_device,
        mesh=mesh,
        in_specs=(rows, rows) + (all_of,) * 4 + state * 4 + frozen + (P(None, "tensor"),),
        out_specs=(rows, rows, all_of) + state * 3,
        check_vma=False,
    )
```

```python
import jax
import jax.numpy as jnp
from jax import lax
from jax.experimental import pallas as pl
from jax.experimental.pallas import tpu as pltpu
from jax.sharding import PartitionSpec as P

D = 2048
HD = 128
ROT = 32
HALF = 256
STEP = 10


NORM_EPSILON = 1e-05
KTO_BETA = 2.0
ADAM_ONE = 0.9
ADAM_TWO = 0.95
ADAM_EPSILON = 1e-08
DECAY_RATE = 0.1
NORM_RATE = 0.3
ROPE_BASE = 10000.0
MASKED = -1e30

LIGHT = pl.CostEstimate(flops=1, bytes_accessed=1, transcendentals=0)
BF = jnp.bfloat16
F32 = jnp.float32


def dot(a, b, dims):
    return lax.dot_general(a, b, (dims, ((), ())), preferred_element_type=F32)


NN = ((1,), (0,))
NT = ((1,), (1,))
TN = ((0,), (0,))


def dp_shape():
    groups = lax.axis_size("dp")
    pair = 2 if groups % 2 == 0 else 1
    return groups, pair, groups // pair


def pair_swap(value):
    groups, _, _ = dp_shape()
    return lax.ppermute(value, "dp", [(i, i ^ 1) for i in range(groups)])


def dp_place():
    _, pair, _ = dp_shape()
    own = lax.axis_index("dp")
    return own // pair, own % pair


def tensor_swap(value, bit):
    return lax.ppermute(value, "tensor", [(i, i ^ bit) for i in range(lax.axis_size("tensor"))])


def ring_groups():
    _, pair, ring = dp_shape()
    return [[r * pair + p for r in range(ring)] for p in range(pair)]


def gather_ring(piece):
    return lax.all_gather(piece, "dp", axis_index_groups=ring_groups())


def scatter_ring(blocks):
    return lax.psum_scatter(blocks, "dp", axis_index_groups=ring_groups())


def by_side(mine, other, axis):
    _, low = dp_place()
    first, second = jnp.stack([mine, other], axis), jnp.stack([other, mine], axis)
    return jnp.where(low == 0, first, second)


def rows_of(mine, other):
    if other is None:
        return mine
    both = by_side(mine, other, 1)
    return both.reshape((-1,) + both.shape[2:])


def to_ring(kept, came):
    if came is not None:
        kept = (kept.astype(F32) + came.astype(F32)).astype(BF)
    return kept[:, 0]


def columns_of(mine, other):
    both = mine[:, None] if other is None else by_side(mine, other, 1)
    ring, pair, rows, slab = both.shape
    return jnp.moveaxis(both, 2, 0).reshape(rows, ring * pair * slab)


def gather_step(held, bit):
    groups = lax.axis_size("dp")
    came = lax.ppermute(held, "dp", [(i, i ^ bit) for i in range(groups)])
    return jnp.where(
        lax.axis_index("dp") & bit == 0,
        jnp.concatenate([held, came]),
        jnp.concatenate([came, held]),
    )


def gather_small(value):
    groups = lax.axis_size("dp")
    if groups & (groups - 1):
        return lax.all_gather(value, "dp")
    held = value[None]
    bit = 1
    while bit < groups:
        held = gather_step(held, bit)
        bit *= 2
    return held


def sum_small(value, axes):
    for axis in axes:
        size = lax.axis_size(axis)
        if size & (size - 1):
            value = lax.psum(value, axis)
            continue
        bit = 1
        while bit < size:
            value = value + lax.ppermute(value, axis, [(i, i ^ bit) for i in range(size)])
            bit *= 2
    return value


def tensor_near(part):
    part = part.astype(BF)
    low = lax.axis_index("tensor") % 2
    half = part.shape[0] // 2
    kept = lax.dynamic_slice_in_dim(part, low * half, half, 0)
    sent = lax.dynamic_slice_in_dim(part, (1 - low) * half, half, 0)
    return (kept.astype(F32) + tensor_swap(sent, 1).astype(F32)).astype(BF)


def tensor_far(kept):
    return (kept.astype(F32) + tensor_swap(kept, 2).astype(F32)).astype(BF)


def tensor_halves(part, *beside):
    part = part.astype(BF)
    if lax.axis_size("tensor") != 4:
        whole = lax.psum(part, "tensor")
        half = part.shape[0] // 2
        return whole[:half], whole[half:], jnp.zeros((1,), jnp.int32)
    kept = tensor_far(tensor_near(part))
    if beside:
        kept = after(kept, *beside)
    return kept, tensor_swap(kept, 1), (lax.axis_index("tensor") % 2).reshape(1)


def whole_rows(mine, other, low):
    return jnp.where(
        low[0] == 0, jnp.concatenate([mine, other], axis=0), jnp.concatenate([other, mine], axis=0)
    )


def tensor_sum(part):
    return whole_rows(*tensor_halves(part))


def tensor_join(part):
    if lax.axis_size("tensor") != 4:
        return lax.all_gather(part, "tensor")
    me = lax.axis_index("tensor")
    far = tensor_swap(part, 2)
    two = jnp.where(me // 2 == 0, jnp.stack([part, far]), jnp.stack([far, part]))
    near = tensor_swap(two, 1)
    four = jnp.where(me % 2 == 0, jnp.stack([two, near], 1), jnp.stack([near, two], 1))
    return four.reshape((4,) + part.shape)


def normalize(values):
    centre = jnp.mean(values, axis=-1, keepdims=True)
    centred = values - centre
    inverse_scale = lax.rsqrt(jnp.mean(centred * centred, axis=-1, keepdims=True) + NORM_EPSILON)
    return (centred * inverse_scale, inverse_scale)


def normalize_back(upstream, unit, inverse_scale):
    return inverse_scale * (
        upstream
        - jnp.mean(upstream, axis=-1, keepdims=True)
        - unit * jnp.mean(upstream * unit, axis=-1, keepdims=True)
    )


def after(value, *others):
    return lax.optimization_barrier((value,) + others)[0]


def turn_tables(half):
    place = jnp.arange(3 * half, dtype=jnp.int32)
    place = jnp.where(place < 2 * half, place, place - half)
    freqs = ROPE_BASE ** (-jnp.arange(ROT // 2, dtype=F32) * 2.0 / ROT)
    angles = place.astype(F32)[:, None] * freqs[None, :]
    cosines, sines = jnp.cos(angles), jnp.sin(angles)
    rest = jnp.zeros((3 * half, HD - ROT), F32)
    none = jnp.zeros_like(sines)
    return jnp.stack(
        [
            jnp.concatenate([cosines, cosines, rest + 1.0], axis=1),
            jnp.concatenate([-sines, none, rest], axis=1),
            jnp.concatenate([none, sines, rest], axis=1),
        ]
    )


def turned(x, table, way):
    step = ROT // 2
    moved = pltpu.roll(x, HD - step, 1) * table[1] + pltpu.roll(x, step, 1) * table[2]
    return x * table[0] + moved * way


def seen_scores(query, near, far, half):
    scale = HD ** (-0.5)
    rows = lax.broadcasted_iota(jnp.int32, (half, half), 0)
    cols = lax.broadcasted_iota(jnp.int32, (half, half), 1)
    own = jnp.where(cols <= rows, dot(query, near, NT) * scale, MASKED)
    peak = jnp.max(own, axis=1, keepdims=True)
    if far is None:
        own = jnp.exp(own - peak)
        return own / jnp.sum(own, axis=1, keepdims=True), None
    before = dot(query, far, NT) * scale
    peak = jnp.maximum(peak, jnp.max(before, axis=1, keepdims=True))
    own, before = jnp.exp(own - peak), jnp.exp(before - peak)
    total = jnp.sum(own, axis=1, keepdims=True) + jnp.sum(before, axis=1, keepdims=True)
    return own / total, before / total


def attend_body(half, skip, x_ref, w_ref, t_ref, out_ref, q_ref, k_ref, v_ref):
    x = x_ref[...]
    raw = [dot(x[skip:], w_ref[0], NN), dot(x, w_ref[1], NN), dot(x, w_ref[2], NN)]
    for h in range(w_ref.shape[2] // HD):
        at = slice(h * HD, (h + 1) * HD)
        query = turned(raw[0][:, at], t_ref[:, skip:], 1.0).astype(BF)
        keys = turned(raw[1][:, at], t_ref[...], 1.0).astype(BF)
        values = raw[2][:, at].astype(BF)
        q_ref[:, at], k_ref[:, at], v_ref[:, at] = query, keys, values
        part = lambda x, g, gone=0: x[g * half - gone : (g + 1) * half - gone]
        for g in range(skip // half, 3):
            own, before = seen_scores(
                part(query, g, skip), part(keys, g), part(keys, 0) if g else None, half
            )
            seen = dot(own.astype(BF), part(values, g), NN)
            if g:
                seen = seen + dot(before.astype(BF), part(values, 0), NN)
            out_ref[g * half - skip : (g + 1) * half - skip, at] = seen.astype(BF)


def head_pairs(inner):
    return 2 * HD if inner % (2 * HD) == 0 else HD


def attention(first_in, weights, tables, half, skip):
    count, width = first_in.shape
    inner = weights.shape[2]
    block = head_pairs(inner)
    columns = lambda rows: pl.BlockSpec((rows, block), lambda h: (0, h))
    shape = lambda rows: jax.ShapeDtypeStruct((rows, inner), BF)
    return pl.pallas_call(
        lambda *refs: attend_body(half, skip, *refs),
        grid=(inner // block,),
        in_specs=[
            pl.BlockSpec((count, width), lambda h: (0, 0)),
            pl.BlockSpec((3, width, block), lambda h: (0, 0, h)),
            pl.BlockSpec(tables.shape, lambda h: (0, 0, 0)),
        ],
        out_specs=[columns(count - skip), columns(count - skip), columns(count), columns(count)],
        out_shape=[shape(count - skip), shape(count - skip), shape(count), shape(count)],
        compiler_params=pltpu.CompilerParams(vmem_limit_bytes=48 * 2**20),
        cost_estimate=LIGHT,
        name="attend",
    )(first_in, weights, tables)


def attend_back_body(half, d_ref, q_ref, k_ref, v_ref, t_ref, out_ref):
    scale = HD ** (-0.5)
    for h in range(d_ref.shape[1] // HD):
        at = slice(h * HD, (h + 1) * HD)
        part = lambda ref, g: ref[g * half : (g + 1) * half, at]
        back_keys = back_values = None
        for g in (1, 2):
            query, far, near = part(q_ref, g), part(k_ref, 0), part(k_ref, g)
            upstream = part(d_ref, g - 1)
            own, before = seen_scores(query, near, far, half)
            own_pull = dot(upstream, part(v_ref, g), NT)
            far_pull = dot(upstream, part(v_ref, 0), NT)
            mean = jnp.sum(own * own_pull, axis=1, keepdims=True) + jnp.sum(
                before * far_pull, axis=1, keepdims=True
            )
            own_back = (own * (own_pull - mean)).astype(BF)
            far_back = (before * (far_pull - mean)).astype(BF)
            back_query = (dot(own_back, near, NN) + dot(far_back, far, NN)) * scale
            rows = slice(g * half, (g + 1) * half)
            out_ref[0, rows, at] = turned(
                back_query, t_ref[:, rows], -1.0
            ).astype(BF)
            out_ref[1, rows, at] = turned(
                dot(own_back, query, TN) * scale, t_ref[:, rows], -1.0
            ).astype(BF)
            out_ref[2, rows, at] = dot(own.astype(BF), upstream, TN).astype(BF)
            more_keys, more_values = dot(far_back, query, TN), dot(before.astype(BF), upstream, TN)
            back_keys = more_keys if back_keys is None else back_keys + more_keys
            back_values = more_values if back_values is None else back_values + more_values
        out_ref[0, :half, at] = jnp.zeros((half, HD), BF)
        out_ref[1, :half, at] = turned(back_keys * scale, t_ref[:, :half], -1.0).astype(BF)
        out_ref[2, :half, at] = back_values.astype(BF)


def attention_back(back_attended, query, keys, values, tables, half):
    count, inner = keys.shape
    block = head_pairs(inner)
    columns = lambda rows: pl.BlockSpec((rows, block), lambda h: (0, h))
    return pl.pallas_call(
        lambda *refs: attend_back_body(half, *refs),
        grid=(inner // block,),
        in_specs=[
            columns(count - half),
            columns(count),
            columns(count),
            columns(count),
            pl.BlockSpec(tables.shape, lambda h: (0, 0, 0)),
        ],
        out_specs=pl.BlockSpec((3, count, block), lambda h: (0, 0, h)),
        out_shape=jax.ShapeDtypeStruct((3, count, inner), BF),
        compiler_params=pltpu.CompilerParams(vmem_limit_bytes=48 * 2**20),
        cost_estimate=LIGHT,
        name="attend_back",
    )(back_attended, query, keys, values, tables)


def hidden_body(skip, before, out_ref, *slope_ref):
    share = 0.5 + 0.5 * lax.erf(before * 0.5**0.5)
    out_ref[...] = (before * share).astype(BF)
    if slope_ref:
        kept = before[skip:]
        bell = jnp.exp(-0.5 * kept * kept) * (2.0 * jnp.pi) ** (-0.5)
        slope_ref[0][...] = share[skip:] + kept * bell


def over_shards(pair, low_ref, x_ref, w_refs, rows_first):
    total = None
    ring = w_refs[0].shape[0]
    slab = w_refs[0].shape[1 if rows_first else 2]
    for side in range(pair):
        for r in range(ring):
            at = pl.multiple_of(shard_of(r, side, low_ref, pair) * slab, slab)
            term = dot(x_ref[:, pl.ds(at, slab)], w_refs[side][r], NN if rows_first else NT)
            total = term if total is None else total + term
    return total


def hidden_units(second_in, expand, skip=None):
    count, width = second_in.shape
    pair = dp_shape()[1]
    if isinstance(expand, tuple) and expand[0].shape[1] % 128:
        expand = rows_of(*expand).reshape(width, -1)
    sides = isinstance(expand, tuple)
    units = expand[0].shape[2] if sides else expand.shape[1]
    block = 256
    column = lambda rows: pl.BlockSpec((rows, block), lambda i, l: (0, i))
    weights = list(expand[:pair]) if sides else [expand]
    weight_specs = [
        pl.BlockSpec(x.shape[:2] + (block,), lambda i, l: (0, 0, i)) if sides else column(width)
        for x in weights
    ]
    out_specs, out_shape = [column(count)], [jax.ShapeDtypeStruct((count, units), BF)]
    if skip is not None:
        out_specs.append(column(count - skip))
        out_shape.append(jax.ShapeDtypeStruct((count - skip, units), F32))

    def body(low_ref, x_ref, *refs):
        w_refs, out_refs = refs[: len(weights)], refs[len(weights) :]
        if sides:
            before = over_shards(pair, low_ref, x_ref, w_refs, True)
        else:
            before = dot(x_ref[...], w_refs[0][...], NN)
        hidden_body(skip, before, *out_refs)

    return pl.pallas_call(
        body,
        grid_spec=pltpu.PrefetchScalarGridSpec(
            num_scalar_prefetch=1,
            grid=(units // block,),
            in_specs=[pl.BlockSpec((count, width), lambda i, l: (0, 0)), *weight_specs],
            out_specs=out_specs,
        ),
        out_shape=out_shape,
        compiler_params=pltpu.CompilerParams(vmem_limit_bytes=48 * 2**20),
        cost_estimate=LIGHT,
        name="hidden",
    )(dp_place()[1].reshape(1), second_in, *weights)


def pull_units(branch_low, weights, slope=None):
    rows, width = branch_low.shape
    pair = dp_shape()[1]
    units, slab = weights[0].shape[1:]
    if slab % 128:
        out = dot(branch_low, columns_of(*weights), NT)
        return (out if slope is None else out * slope).astype(BF)
    block = 256
    weights = list(weights[:pair])
    column = pl.BlockSpec((rows, block), lambda i, l: (0, i))

    def body(low_ref, x_ref, *refs):
        out = over_shards(pair, low_ref, x_ref, refs[:pair], False)
        if slope is not None:
            out = out * refs[pair][...]
        refs[-1][...] = out.astype(BF)

    return pl.pallas_call(
        body,
        grid_spec=pltpu.PrefetchScalarGridSpec(
            num_scalar_prefetch=1,
            grid=(units // block,),
            in_specs=[
                pl.BlockSpec((rows, width), lambda i, l: (0, 0)),
                *(
                    pl.BlockSpec((x.shape[0], block, slab), lambda i, l: (0, i, 0))
                    for x in weights
                ),
                *([] if slope is None else [column]),
            ],
            out_specs=column,
        ),
        out_shape=jax.ShapeDtypeStruct((rows, units), BF),
        compiler_params=pltpu.CompilerParams(vmem_limit_bytes=48 * 2**20),
        cost_estimate=LIGHT,
        name="pull_units",
    )(dp_place()[1].reshape(1), branch_low, *weights, *([] if slope is None else [slope]))


def shard_of(r, side, low, pair):
    return r * pair + (low[0] + side) % pair


def grad_body(x_ref, y_ref, out_ref):
    x = x_ref[...]
    for i in range(y_ref.shape[0]):
        out_ref[0, 0, i] = dot(x, y_ref[i], TN).astype(BF)


def grad_blocks(left, right, sides):
    groups, pair, ring = dp_shape()
    low = dp_place()[1].reshape(1)
    rows = left.shape[0]
    slab = left.shape[1] // groups
    parts, _, width = right.shape
    if slab % 128:
        shards = left.reshape(rows, ring, pair, slab)
        shards = jnp.stack([shards[:, :, (low[0] + s) % pair] for s in sides], axis=2)
        out = jnp.einsum("nrsc,pnw->rspcw", shards, right, preferred_element_type=F32)
        return out.astype(BF)
    first = sides[0]
    return pl.pallas_call(
        lambda low_ref, *refs: grad_body(*refs),
        grid_spec=pltpu.PrefetchScalarGridSpec(
            num_scalar_prefetch=1,
            grid=(ring, len(sides)),
            in_specs=[
                pl.BlockSpec((rows, slab), lambda r, s, l: (0, shard_of(r, s + first, l, pair))),
                pl.BlockSpec(right.shape, lambda r, s, l: (0, 0, 0)),
            ],
            out_specs=pl.BlockSpec(
                (1, 1, parts, slab, width), lambda r, s, l: (r, s, 0, 0, 0)
            ),
        ),
        out_shape=jax.ShapeDtypeStruct((ring, len(sides), parts, slab, width), BF),
        compiler_params=pltpu.CompilerParams(vmem_limit_bytes=48 * 2**20),
        cost_estimate=LIGHT,
        name="grad_blocks",
    )(low, left, right)


def branch_terms(hidden, attended, contract, attend_out, blocks, half):
    groups, pair, ring = dp_shape()
    low = dp_place()[1].reshape(1)
    slab = contract[0].shape[2]
    count = half * len(blocks)
    if slab % 128:
        rows = slice(blocks[0] * half, blocks[0] * half + count)
        out = 0.0
        for x, sides in ((hidden[rows], contract), (attended[rows], attend_out)):
            if pair == 2:
                sides = [by_side(sides[0], sides[1], 1)]
            weight = sides[0].reshape(groups, x.shape[1], slab)
            out = out + jnp.einsum("nf,sfc->nsc", x, weight, preferred_element_type=F32)
        return out.reshape(count, groups * slab).astype(BF)
    weights = [*contract[:pair], *attend_out[:pair]]
    row_block = lambda x, b: pl.BlockSpec((half, x.shape[1]), lambda r, s, l: (b, 0))

    def body(low_ref, *refs):
        x_refs, refs = refs[: 2 * len(blocks)], refs[2 * len(blocks) :]

        def write(side):
            for i in range(len(blocks)):
                refs[-1][i * half : (i + 1) * half] = (
                    dot(x_refs[2 * i][...], refs[side][0], NN)
                    + dot(x_refs[2 * i + 1][...], refs[pair + side][0], NN)
                ).astype(BF)

        for side in range(pair):
            pl.when(pl.program_id(1) == side)(lambda: write(side))

    return pl.pallas_call(
        body,
        grid_spec=pltpu.PrefetchScalarGridSpec(
            num_scalar_prefetch=1,
            grid=(ring, pair),
            in_specs=[
                *(row_block(x, b) for b in blocks for x in (hidden, attended)),
                *(pl.BlockSpec((1,) + x.shape[1:], lambda r, s, l: (r, 0, 0)) for x in weights),
            ],
            out_specs=pl.BlockSpec(
                (count, slab), lambda r, s, l: (0, shard_of(r, s, l, pair))
            ),
        ),
        out_shape=jax.ShapeDtypeStruct((count, groups * slab), BF),
        compiler_params=pltpu.CompilerParams(vmem_limit_bytes=48 * 2**20),
        cost_estimate=LIGHT,
        name="branch",
    )(low, *[hidden, attended] * len(blocks), *weights)


def shard_terms(lefts, weights):
    groups, pair, ring = dp_shape()
    low = dp_place()[1].reshape(1)
    weights = list(weights[:pair])
    count = lefts.shape[1]
    parts, slab, depth = weights[0].shape[1:]
    if slab % 128:
        whole = by_side(weights[0], weights[1], 1) if pair == 2 else weights[0]
        whole = whole.reshape(groups, parts, slab, depth)
        out = jnp.einsum("pnk,gpsk->ngs", lefts, whole, preferred_element_type=F32)
        return out.reshape(count, groups * slab)

    def body(low_ref, x_ref, *refs):
        def write(side):
            total = dot(x_ref[0], refs[side][0, 0], NT)
            for i in range(1, parts):
                total = total + dot(x_ref[i], refs[side][0, i], NT)
            refs[-1][...] = total

        for side in range(pair):
            pl.when(pl.program_id(1) == side)(lambda: write(side))

    return pl.pallas_call(
        body,
        grid_spec=pltpu.PrefetchScalarGridSpec(
            num_scalar_prefetch=1,
            grid=(ring, pair),
            in_specs=[
                pl.BlockSpec(lefts.shape, lambda r, s, l: (0, 0, 0)),
                *(pl.BlockSpec((1,) + x.shape[1:], lambda r, s, l: (r, 0, 0, 0)) for x in weights),
            ],
            out_specs=pl.BlockSpec(
                (count, slab), lambda r, s, l: (0, shard_of(r, s, l, pair))
            ),
        ),
        out_shape=jax.ShapeDtypeStruct((count, groups * slab), F32),
        compiler_params=pltpu.CompilerParams(vmem_limit_bytes=48 * 2**20),
        cost_estimate=LIGHT,
        name="shard_terms",
    )(low, lefts, *weights)


def out_body(x_ref, mine_ref, other_ref, low_ref, unit_ref, low_unit_ref, scale_ref, out_ref):
    mine = pl.program_id(0) == low_ref[0]
    branch = jnp.where(mine, mine_ref[...].astype(F32), other_ref[...].astype(F32))
    out = x_ref[...].astype(F32) + branch
    unit, scale = normalize(out)
    unit_ref[...] = unit
    low_unit_ref[...] = unit.astype(BF)
    scale_ref[...] = scale
    out_ref[...] = out.astype(BF)


def out_rows(x, halves):
    mine, other, low = halves
    rows, width = x.shape
    block = 128
    steps = rows // 2 // block
    whole = pl.BlockSpec((block, width), lambda h, i: (h * steps + i, 0))
    part = pl.BlockSpec((block, width), lambda h, i: (i, 0))
    return pl.pallas_call(
        out_body,
        grid=(2, steps),
        in_specs=[whole, part, part, pl.BlockSpec(memory_space=pltpu.SMEM)],
        out_specs=[whole, whole, pl.BlockSpec((block, 1), lambda h, i: (h * steps + i, 0)), whole],
        out_shape=[
            jax.ShapeDtypeStruct((rows, width), F32),
            jax.ShapeDtypeStruct((rows, width), BF),
            jax.ShapeDtypeStruct((rows, 1), F32),
            jax.ShapeDtypeStruct((rows, width), BF),
        ],
        compiler_params=pltpu.CompilerParams(vmem_limit_bytes=48 * 2**20),
        cost_estimate=LIGHT,
        name="out_rows",
    )(x, mine, other, low)


def pull_body(mine_ref, other_ref, low_ref, weight_ref, unit_ref, scale_ref, out_ref, low_out_ref):
    mine = pl.program_id(0) == low_ref[0]
    upstream = jnp.where(mine, mine_ref[...].astype(F32), other_ref[...].astype(F32))
    out = normalize_back(upstream * weight_ref[...], unit_ref[...], scale_ref[...])
    out_ref[...] = out
    low_out_ref[...] = out.astype(BF)


def pull_rows(halves, weight, unit, scale):
    mine, other, low = halves
    rows, width = unit.shape
    block = 128
    steps = rows // 2 // block
    whole = lambda columns: pl.BlockSpec((block, columns), lambda h, i: (h * steps + i, 0))
    part = pl.BlockSpec((block, width), lambda h, i: (i, 0))
    return pl.pallas_call(
        pull_body,
        grid=(2, steps),
        in_specs=[
            part,
            part,
            pl.BlockSpec(memory_space=pltpu.SMEM),
            whole(1),
            whole(width),
            whole(1),
        ],
        out_specs=[whole(width), whole(width)],
        out_shape=[
            jax.ShapeDtypeStruct((rows, width), F32),
            jax.ShapeDtypeStruct((rows, width), BF),
        ],
        compiler_params=pltpu.CompilerParams(vmem_limit_bytes=48 * 2**20),
        cost_estimate=LIGHT,
        name="pull_rows",
    )(mine, other, low, weight, unit, scale)


def borrow_rows(tail, order, first=(), last=()):
    groups = lax.axis_size("dp")
    parts = lax.axis_size("tensor")
    count, rows, width = tail.shape
    share = rows // parts
    mine = lax.dynamic_slice_in_dim(tail, lax.axis_index("tensor") * share, share, 1)
    mine = mine.reshape(count, groups, share // groups, width).swapaxes(0, 1)
    spread = after(lax.all_to_all(mine, "dp", split_axis=0, concat_axis=0, tiled=True), *first)
    landed = lax.all_to_all(
        jnp.take(spread, order, axis=0), "dp", split_axis=0, concat_axis=0, tiled=True
    )
    landed = landed.swapaxes(0, 1).reshape(count, share, width)
    return tensor_join(after(landed, *last)).swapaxes(0, 1).reshape(count, rows, width)


TILE = 1280
CHUNK = 256
PULL_CHUNK = 640


def head_body(vocab, x_ref, w_ref, t_ref, *refs):
    logits_ref, stats_ref, peak_ref, total_ref, picked_ref = refs if len(refs) == 5 else (None, *refs)
    step = pl.program_id(0)

    @pl.when(step == 0)
    def _():
        peak_ref[...] = jnp.full(peak_ref.shape, MASKED, F32)
        total_ref[...] = jnp.zeros(total_ref.shape, F32)
        picked_ref[...] = jnp.zeros(picked_ref.shape, F32)

    x, target = x_ref[...], t_ref[...]
    lanes = lax.broadcasted_iota(jnp.int32, (x.shape[0], 128), 1)
    for c in range(0, TILE, CHUNK):
        logits = dot(x, w_ref[c : c + CHUNK], NT)
        if logits_ref is not None:
            logits_ref[:, c : c + CHUNK] = logits
        parts = []
        picked = picked_ref[...]
        for d in range(0, CHUNK, 128):
            column = lanes + (step * TILE + c + d)
            part = jnp.where(column < vocab, logits[:, d : d + 128], MASKED)
            picked = picked + jnp.where(column == target, part, 0.0)
            parts.append(part)
        picked_ref[...] = picked
        old = peak_ref[...]
        peak = old
        for part in parts:
            peak = jnp.maximum(peak, part)
        total = total_ref[...] * jnp.exp(old - peak)
        for part in parts:
            total = total + jnp.exp(part - peak)
        peak_ref[...] = peak
        total_ref[...] = total

    @pl.when(step == pl.num_programs(0) - 1)
    def _():
        peak = jnp.max(peak_ref[...], axis=1, keepdims=True)
        total = jnp.sum(total_ref[...] * jnp.exp(peak_ref[...] - peak), axis=1, keepdims=True)
        picked = jnp.sum(picked_ref[...], axis=1, keepdims=True)
        rows = jnp.where(lanes == 0, peak, jnp.where(lanes == 1, total, picked))
        stats_ref[...] = rows.T[:8]


def head_stats(unit_low, table, local_targets, keep):
    rows, width = unit_low.shape
    vocab = table.shape[0]
    tiles = pl.cdiv(vocab, TILE)
    out_specs = [pl.BlockSpec((8, rows), lambda i: (0, 0))]
    out_shape = [jax.ShapeDtypeStruct((8, rows), F32)]
    if keep:
        out_specs.insert(0, pl.BlockSpec((rows, TILE), lambda i: (0, i)))
        out_shape.insert(0, jax.ShapeDtypeStruct((rows, vocab), F32))
    out = pl.pallas_call(
        lambda *refs: head_body(vocab, *refs),
        grid=(tiles,),
        in_specs=[
            pl.BlockSpec((rows, width), lambda i: (0, 0)),
            pl.BlockSpec((TILE, width), lambda i: (i, 0)),
            pl.BlockSpec((rows, 1), lambda i: (0, 0)),
        ],
        out_specs=out_specs,
        out_shape=out_shape,
        scratch_shapes=[pltpu.VMEM((rows, 128), F32)] * 3,
        compiler_params=pltpu.CompilerParams(vmem_limit_bytes=48 * 2**20),
        cost_estimate=LIGHT,
        name="head",
    )(unit_low, table, local_targets[:, None])
    return out[-1][:3], out[0] if keep else None


def head_pull_body(vocab, tiles, x_ref, w_ref, row_ref, t_ref, out_ref, pull_ref, total_ref):
    step = pl.program_id(0)

    @pl.when(step == 0)
    def _():
        total_ref[...] = jnp.zeros(total_ref.shape, F32)

    def add(masked):
        for c in range(0, TILE, PULL_CHUNK):
            at = slice(c, c + PULL_CHUNK)
            column = lax.broadcasted_iota(jnp.int32, (x_ref.shape[0], PULL_CHUNK), 1)
            column = column + (step * TILE + c)
            pull = jnp.where(column == t_ref[...], 1.0, 0.0) - jnp.exp(
                x_ref[:, at] - row_ref[:, 0:1]
            ) * row_ref[:, 1:2]
            if masked:
                pull = jnp.where(column < vocab, pull, 0.0)
            pull_ref[:, at] = pull.astype(BF)
        width = w_ref.shape[1]
        for c in range(0, width, width // 4):
            at = slice(c, c + width // 4)
            weight = w_ref[:, at]
            if masked:
                seen = lax.broadcasted_iota(jnp.int32, weight.shape, 0)
                seen = seen < vocab - (tiles - 1) * TILE
                weight = jnp.where(seen, weight.astype(F32), 0.0).astype(BF)
            total_ref[:, at] += dot(pull_ref[...], weight, NN)

    pl.when(step < tiles - 1)(lambda: add(False))
    pl.when(step == tiles - 1)(lambda: add(True))

    @pl.when(step == tiles - 1)
    def _():
        out_ref[...] = total_ref[...].astype(BF)


def head_pull(logits, table, row, targets):
    rows, vocab = logits.shape
    width = table.shape[1]
    tiles = pl.cdiv(vocab, TILE)
    whole = lambda x: pl.BlockSpec(x, lambda i: (0, 0))
    return pl.pallas_call(
        lambda *refs: head_pull_body(vocab, tiles, *refs),
        grid=(tiles,),
        in_specs=[
            pl.BlockSpec((rows, TILE), lambda i: (0, i)),
            pl.BlockSpec((TILE, width), lambda i: (i, 0)),
            whole((rows, 2)),
            whole((rows, 1)),
        ],
        out_specs=whole((rows, width)),
        out_shape=jax.ShapeDtypeStruct((rows, width), BF),
        scratch_shapes=[pltpu.VMEM((rows, TILE), BF), pltpu.VMEM((rows, width), F32)],
        compiler_params=pltpu.CompilerParams(vmem_limit_bytes=48 * 2**20),
        cost_estimate=LIGHT,
        name="head_pull",
    )(logits, table, row, targets[:, None])


def join_stats(stats):
    every = lax.all_gather(stats, "tensor")
    peak = jnp.max(every[:, 0], axis=0)
    total = jnp.sum(every[:, 1] * jnp.exp(every[:, 0] - peak[None]), axis=0)
    return peak, total, jnp.sum(every[:, 2], axis=0)


def adamw_step(master, first, second, gradient, rate, decay):
    new_first = ADAM_ONE * first + (1.0 - ADAM_ONE) * gradient
    new_second = ADAM_TWO * second + (1.0 - ADAM_TWO) * gradient * gradient
    ratio = (
        new_first
        / (1.0 - ADAM_ONE**STEP)
        / (jnp.sqrt(new_second / (1.0 - ADAM_TWO**STEP)) + ADAM_EPSILON)
    )
    return (master - rate * (ratio + decay * master), new_first, new_second)


def per_device(
    policy_rows,
    frozen_rows,
    next_tokens,
    desirable,
    answer_len,
    partner,
    norms_copy,
    attend_in_copy,
    attend_out_copy,
    expand_copy,
    contract_copy,
    norms_master,
    attend_in_master,
    attend_out_master,
    expand_master,
    contract_master,
    norms_first,
    attend_in_first,
    attend_out_first,
    expand_first,
    contract_first,
    norms_second,
    attend_in_second,
    attend_out_second,
    expand_second,
    contract_second,
    frozen_norms,
    frozen_in,
    frozen_out,
    frozen_expand,
    frozen_contract,
    vocab_table,
):
    groups = lax.axis_size("dp")
    own_index = lax.axis_index("dp")
    half = policy_rows.shape[0] // 2
    inner = attend_in_copy.shape[2]
    slab = attend_in_copy.shape[1]
    width = policy_rows.shape[1]
    inverse = jnp.zeros_like(partner).at[partner].set(jnp.arange(groups, dtype=jnp.int32))
    other_index = partner[own_index]

    norms_full = gather_small(norms_copy).swapaxes(0, 1).reshape(4, width).astype(F32)
    units = expand_copy.shape[1]
    _, pair, ring = dp_shape()
    _, low = dp_place()
    swap = pair_swap if pair == 2 else (lambda value: None)
    cut = (units + inner) // 2
    out_came = swap(attend_out_copy)
    attend_mine = gather_ring(attend_in_copy)
    expand_mine = gather_ring(expand_copy)
    contract_mine = gather_ring(contract_copy)
    out_mine = gather_ring(attend_out_copy)
    out_other = None if out_came is None else gather_ring(out_came)
    norms_full = norms_full if out_came is None else after(norms_full, out_came)

    other = borrow_rows(jnp.stack([frozen_rows[half:], policy_rows[half:]]), partner)
    other, attend_mine = lax.optimization_barrier((other, attend_mine))
    tables = turn_tables(half)

    frozen_work = jnp.concatenate([frozen_rows, other[0]], axis=0).astype(F32)
    frozen_unit, _ = normalize(frozen_work)
    frozen_first_in = (frozen_unit * frozen_norms[0] + frozen_norms[1]).astype(BF)
    frozen_second_in = (frozen_unit[half:] * frozen_norms[2] + frozen_norms[3]).astype(BF)
    frozen_first_in, frozen_second_in, norms_full = lax.optimization_barrier(
        (frozen_first_in, frozen_second_in, norms_full)
    )
    attend_other = swap(attend_mine)
    frozen_attended = attention(frozen_first_in, frozen_in, tables, half, half)[0]
    (frozen_hidden,) = hidden_units(frozen_second_in, frozen_expand)
    frozen_part = dot(frozen_attended, frozen_out, NN) + dot(frozen_hidden, frozen_contract, NN)
    frozen_part, attend_other, expand_mine = lax.optimization_barrier(
        (frozen_part.astype(BF), attend_other, expand_mine)
    )
    expand_other = swap(expand_mine)
    frozen_low = out_rows(
        jnp.concatenate([frozen_rows[half:], other[0]], axis=0), tensor_halves(frozen_part)
    )[1]
    vocab_local = vocab_table.shape[1]
    table = vocab_table.T
    targets = (
        jnp.concatenate([next_tokens[own_index], next_tokens[other_index]])
        - lax.axis_index("tensor") * vocab_local
    )
    targets = jnp.where((targets >= 0) & (targets < vocab_local), targets, -1)
    work = jnp.concatenate([policy_rows, other[1]], axis=0).astype(F32)
    unit, inverse_scale = normalize(work)
    first_in = (unit * norms_full[0] + norms_full[1]).astype(BF)
    second_in = (unit * norms_full[2] + norms_full[3]).astype(BF)
    attend_in = rows_of(attend_mine, attend_other)
    attend_in = attend_in.swapaxes(0, 1).reshape(3, width, inner)
    attended, query, keys, values = attention(first_in, attend_in, tables, half, 0)
    second_in, contract_mine, attended, expand_other = lax.optimization_barrier(
        (second_in, contract_mine, attended, expand_other)
    )
    contract_other = swap(contract_mine)
    frozen_low, second_in = lax.optimization_barrier((frozen_low, second_in))
    frozen_stats, _ = head_stats(frozen_low, table, targets, False)
    frozen_peak, frozen_total, frozen_picked = join_stats(frozen_stats)
    second_in, frozen_peak = lax.optimization_barrier((second_in, frozen_peak))
    hidden, slope_units = hidden_units(second_in, (expand_mine, expand_other), half)

    contract, attend_out = (contract_mine, contract_other), (out_mine, out_other)
    scored_halves = tensor_halves(
        branch_terms(hidden, attended, contract, attend_out, (1, 2), half)
    )
    unit_out, unit_low, inverse_out, out_low = out_rows(
        jnp.concatenate([policy_rows[half:], other[1]], axis=0), scored_halves
    )
    stats, logits = head_stats(unit_low, table, targets, True)
    peak, total, picked = join_stats(stats)
    log_chance = jnp.stack(
        [picked - peak - jnp.log(total), frozen_picked - frozen_peak - jnp.log(frozen_total)]
    )
    steps = jnp.arange(half, dtype=jnp.int32)
    own_count = answer_len[own_index]
    other_count = answer_len[other_index]
    own_live = (steps < own_count).astype(F32)
    other_live = (steps < other_count).astype(F32)
    own_total = own_count.astype(F32)
    other_total = other_count.astype(F32)
    own_mean = jnp.sum(log_chance[:, :half] * own_live, axis=1) / own_total
    other_mean = jnp.sum(log_chance[:, half:] * other_live, axis=1) / other_total
    gaps = jnp.stack([own_mean[0] - own_mean[1], other_mean[0] - other_mean[1]])
    row = jnp.stack([peak, 1.0 / total], axis=1)
    every = gather_small(gaps)
    back_part = head_pull(logits, table, row, targets)
    drift = jnp.sum(every[:, 1]) / groups
    sign = (2 * desirable - 1).astype(F32)
    settled = jax.nn.sigmoid(KTO_BETA * sign * (every[:, 0] - jax.nn.softplus(drift)))
    slope = KTO_BETA * sign * settled * (1.0 - settled)
    loss_total = jnp.sum(1.0 - settled)
    pull = jnp.sum(slope) * jax.nn.sigmoid(drift) / groups
    row_weight = jnp.concatenate(
        [-slope[own_index] * own_live / own_total, pull * other_live / other_total]
    )

    back_sum = tensor_halves(back_part, row_weight)
    back_out, branch_low = pull_rows(back_sum, row_weight[:, None], unit_out, inverse_out)

    features_scored = jnp.concatenate([hidden[half:], attended[half:]], axis=1)
    near_features, far_features = features_scored[:, :cut][None], features_scored[:, cut:][None]
    near_sent = grad_blocks(branch_low, near_features, (1,))
    near_came = swap(near_sent)
    branch_low = after(branch_low, near_sent)
    far_blocks = grad_blocks(branch_low, far_features, range(pair))
    far_back = scatter_ring(far_blocks)

    branch_low = after(branch_low, far_blocks)
    back_expand = pull_units(branch_low, contract, slope_units)
    expand_sent = grad_blocks(second_in[half:], back_expand[None], (1,))
    near_kept = grad_blocks(after(branch_low, expand_sent), near_features, (0,))
    near_ring = to_ring(near_kept, near_came)
    grad_near = scatter_ring(near_ring)[0].astype(F32)

    expand_sent, branch_low, back_expand, near_ring = lax.optimization_barrier(
        (expand_sent, branch_low, back_expand, near_ring)
    )
    expand_came = swap(expand_sent)
    back_attended = pull_units(branch_low, attend_out)
    back_three = attention_back(back_attended, query, keys, values, tables, half)
    attend_sent = grad_blocks(first_in, back_three, (1,))
    sided = lambda sides: [x if x is None else x[:, None] for x in sides]
    back_second = shard_terms(back_expand[None], sided((expand_mine, expand_other)))
    back_first = shard_terms(back_three, (attend_mine, attend_other))

    unit_scored = unit[half:]
    grad_norms = sum_small(
        jnp.stack(
            [
                jnp.sum(back_first * unit, axis=0),
                jnp.sum(back_first, axis=0),
                jnp.sum(back_second * unit_scored, axis=0),
                jnp.sum(back_second, axis=0),
            ]
        ),
        ("tensor",),
    )
    back_h = back_first * norms_full[0] + jnp.pad(
        back_second * norms_full[2], ((half, 0), (0, 0))
    )
    four = lax.axis_size("tensor") == 4
    back_h = tensor_near(back_h) if four else lax.psum(back_h.astype(BF), "tensor")
    second_scored, far_back = lax.optimization_barrier(
        (second_in[half:], far_back, attend_sent, back_h)
    )[:2]
    expand_kept = grad_blocks(second_scored, back_expand[None], (0,))
    expand_ring = to_ring(expand_kept, expand_came)
    expand_back = scatter_ring(expand_ring)

    attend_sent, back_three, expand_ring = lax.optimization_barrier(
        (attend_sent, back_three, expand_ring)
    )
    attend_came = swap(attend_sent)
    attend_kept = grad_blocks(after(first_in, expand_ring), back_three, (0,))
    attend_ring = to_ring(attend_kept, attend_came)
    across = tensor_swap(back_h, 2) if four else back_h
    attend_ring, expand_back, across = lax.optimization_barrier((attend_ring, expand_back, across))
    if four:
        back_h = (back_h.astype(F32) + across.astype(F32)).astype(BF)
        low_row = (lax.axis_index("tensor") % 2).reshape(1)
        back_h = whole_rows(back_h, tensor_swap(back_h, 1), low_row)
    grad_expand = expand_back[0].astype(F32)
    attend_back = scatter_ring(attend_ring)
    hidden = after(hidden, attend_ring)
    back_work = normalize_back(
        back_h.astype(F32), unit, inverse_scale
    ) + jnp.pad(back_out, ((half, 0), (0, 0)))
    out_prompt = work[:half] + tensor_sum(
        branch_terms(hidden, attended, contract, attend_out, (0,), half)
    ).astype(F32)
    mixed = jnp.concatenate([out_prompt.astype(BF), out_low[:half]], axis=0)
    grad_norms = sum_small(after(grad_norms, attend_ring), ("dp",))
    grad_norms = lax.dynamic_slice_in_dim(grad_norms, own_index * slab, slab, 1)
    returned = borrow_rows(back_work[None, 2 * half :].astype(BF), inverse, (attend_ring,), (attend_back,))[0]
    grad_far = far_back[0, 0].astype(F32)
    if pair == 2:
        grad_far = grad_far + pair_swap(after(far_back[1, 0], attend_ring)).astype(F32)
    grad_join = jnp.concatenate([grad_near.T, grad_far.T], axis=0)
    grad_contract, grad_attend_out = grad_join[:units], grad_join[units:]
    input_grad = jnp.concatenate(
        [back_work[:half], back_work[half : 2 * half] + returned.astype(F32)], axis=0
    )

    matrix_rate = 0.5 * D ** (-0.5)
    out_rate = 0.5 * max(D // HALF, 1) ** (-0.5)
    masters = (norms_master, attend_in_master, attend_out_master, expand_master, contract_master)
    firsts = (norms_first, attend_in_first, attend_out_first, expand_first, contract_first)
    seconds = (norms_second, attend_in_second, attend_out_second, expand_second, contract_second)
    rates = (NORM_RATE, matrix_rate, out_rate, matrix_rate, matrix_rate)
    decays = (0.0, DECAY_RATE, DECAY_RATE, DECAY_RATE, DECAY_RATE)
    gradients = [grad_norms, None, grad_attend_out, grad_expand, grad_contract]
    updated = [None] * 5
    for i in (2, 4, 3, 0):
        updated[i] = adamw_step(
            masters[i], firsts[i], seconds[i], gradients[i], rates[i], decays[i]
        )
    attend_back, *waited = lax.optimization_barrier(
        (attend_back, *(updated[i][0] for i in (2, 4, 3, 0)))
    )
    for i, first in zip((2, 4, 3, 0), waited):
        updated[i] = (first,) + updated[i][1:]
    updated[1] = adamw_step(
        masters[1], firsts[1], seconds[1], attend_back.astype(F32), rates[1], decays[1]
    )
    return (
        mixed,
        input_grad,
        jnp.reshape(loss_total, (1,)),
        *(step[0] for step in updated),
        *(step[1] for step in updated),
        *(step[2] for step in updated),
    )


def solution(mesh):
    rows = P("dp", None)
    all_of = P()
    state = (P(None, "dp"), P(None, "dp", "tensor"), P("tensor", "dp"), P("dp", "tensor"), P("tensor", "dp"))
    frozen = (all_of, P(None, None, "tensor"), P("tensor", None), P(None, "tensor"), P("tensor", None))
    return jax.shard_map(
        per_device,
        mesh=mesh,
        in_specs=(rows, rows) + (all_of,) * 4 + state * 4 + frozen + (P(None, "tensor"),),
        out_specs=(rows, rows, all_of) + state * 3,
        check_vma=False,
    )
```

```python
import jax
import jax.numpy as jnp
from jax import lax
from jax.experimental import pallas as pl
from jax.experimental.pallas import tpu as pltpu
from jax.sharding import PartitionSpec as P

D = 2048
HD = 128
ROT = 32
HALF = 256
STEP = 10


NORM_EPSILON = 1e-05
KTO_BETA = 2.0
ADAM_ONE = 0.9
ADAM_TWO = 0.95
ADAM_EPSILON = 1e-08
DECAY_RATE = 0.1
NORM_RATE = 0.3
ROPE_BASE = 10000.0
MASKED = -1e30

LIGHT = pl.CostEstimate(flops=1, bytes_accessed=1, transcendentals=0)
BF = jnp.bfloat16
F32 = jnp.float32


def dot(a, b, dims):
    return lax.dot_general(a, b, (dims, ((), ())), preferred_element_type=F32)


NN = ((1,), (0,))
NT = ((1,), (1,))
TN = ((0,), (0,))


def dp_shape():
    groups = lax.axis_size("dp")
    pair = 2 if groups % 2 == 0 else 1
    return groups, pair, groups // pair


def pair_swap(value):
    groups, _, _ = dp_shape()
    return lax.ppermute(value, "dp", [(i, i ^ 1) for i in range(groups)])


def dp_place():
    _, pair, _ = dp_shape()
    own = lax.axis_index("dp")
    return own // pair, own % pair


def tensor_swap(value, bit):
    return lax.ppermute(value, "tensor", [(i, i ^ bit) for i in range(lax.axis_size("tensor"))])


def ring_groups():
    _, pair, ring = dp_shape()
    return [[r * pair + p for r in range(ring)] for p in range(pair)]


def gather_ring(piece):
    return lax.all_gather(piece, "dp", axis_index_groups=ring_groups())


def scatter_ring(blocks):
    return lax.psum_scatter(blocks, "dp", axis_index_groups=ring_groups())


def by_side(mine, other, axis):
    _, low = dp_place()
    first, second = jnp.stack([mine, other], axis), jnp.stack([other, mine], axis)
    return jnp.where(low == 0, first, second)


def rows_of(mine, other):
    if other is None:
        return mine
    both = by_side(mine, other, 1)
    return both.reshape((-1,) + both.shape[2:])


def to_ring(kept, came):
    if came is not None:
        kept = (kept.astype(F32) + came.astype(F32)).astype(BF)
    return kept[:, 0]


def columns_of(mine, other):
    both = mine[:, None] if other is None else by_side(mine, other, 1)
    ring, pair, rows, slab = both.shape
    return jnp.moveaxis(both, 2, 0).reshape(rows, ring * pair * slab)


def gather_step(held, bit):
    groups = lax.axis_size("dp")
    came = lax.ppermute(held, "dp", [(i, i ^ bit) for i in range(groups)])
    return jnp.where(
        lax.axis_index("dp") & bit == 0,
        jnp.concatenate([held, came]),
        jnp.concatenate([came, held]),
    )


def gather_small(value):
    groups = lax.axis_size("dp")
    if groups & (groups - 1):
        return lax.all_gather(value, "dp")
    held = value[None]
    bit = 1
    while bit < groups:
        held = gather_step(held, bit)
        bit *= 2
    return held


def sum_small(value, axes):
    for axis in axes:
        size = lax.axis_size(axis)
        if size & (size - 1):
            value = lax.psum(value, axis)
            continue
        bit = 1
        while bit < size:
            value = value + lax.ppermute(value, axis, [(i, i ^ bit) for i in range(size)])
            bit *= 2
    return value


def tensor_near(part):
    part = part.astype(BF)
    low = lax.axis_index("tensor") % 2
    half = part.shape[0] // 2
    kept = lax.dynamic_slice_in_dim(part, low * half, half, 0)
    sent = lax.dynamic_slice_in_dim(part, (1 - low) * half, half, 0)
    return (kept.astype(F32) + tensor_swap(sent, 1).astype(F32)).astype(BF)


def tensor_far(kept):
    return (kept.astype(F32) + tensor_swap(kept, 2).astype(F32)).astype(BF)


def tensor_halves(part, *beside):
    part = part.astype(BF)
    if lax.axis_size("tensor") != 4:
        whole = lax.psum(part, "tensor")
        half = part.shape[0] // 2
        return whole[:half], whole[half:], jnp.zeros((1,), jnp.int32)
    kept = tensor_far(tensor_near(part))
    if beside:
        kept = after(kept, *beside)
    return kept, tensor_swap(kept, 1), (lax.axis_index("tensor") % 2).reshape(1)


def whole_rows(mine, other, low):
    return jnp.where(
        low[0] == 0, jnp.concatenate([mine, other], axis=0), jnp.concatenate([other, mine], axis=0)
    )


def tensor_sum(part):
    return whole_rows(*tensor_halves(part))


def tensor_join(part):
    if lax.axis_size("tensor") != 4:
        return lax.all_gather(part, "tensor")
    me = lax.axis_index("tensor")
    far = tensor_swap(part, 2)
    two = jnp.where(me // 2 == 0, jnp.stack([part, far]), jnp.stack([far, part]))
    near = tensor_swap(two, 1)
    four = jnp.where(me % 2 == 0, jnp.stack([two, near], 1), jnp.stack([near, two], 1))
    return four.reshape((4,) + part.shape)


def normalize(values):
    centre = jnp.mean(values, axis=-1, keepdims=True)
    centred = values - centre
    inverse_scale = lax.rsqrt(jnp.mean(centred * centred, axis=-1, keepdims=True) + NORM_EPSILON)
    return (centred * inverse_scale, inverse_scale)


def normalize_back(upstream, unit, inverse_scale):
    return inverse_scale * (
        upstream
        - jnp.mean(upstream, axis=-1, keepdims=True)
        - unit * jnp.mean(upstream * unit, axis=-1, keepdims=True)
    )


def after(value, *others):
    return lax.optimization_barrier((value,) + others)[0]


def turn_tables(half):
    place = jnp.arange(3 * half, dtype=jnp.int32)
    place = jnp.where(place < 2 * half, place, place - half)
    freqs = ROPE_BASE ** (-jnp.arange(ROT // 2, dtype=F32) * 2.0 / ROT)
    angles = place.astype(F32)[:, None] * freqs[None, :]
    cosines, sines = jnp.cos(angles), jnp.sin(angles)
    rest = jnp.zeros((3 * half, HD - ROT), F32)
    none = jnp.zeros_like(sines)
    return jnp.stack(
        [
            jnp.concatenate([cosines, cosines, rest + 1.0], axis=1),
            jnp.concatenate([-sines, none, rest], axis=1),
            jnp.concatenate([none, sines, rest], axis=1),
        ]
    )


def turned(x, table, way):
    step = ROT // 2
    moved = pltpu.roll(x, HD - step, 1) * table[1] + pltpu.roll(x, step, 1) * table[2]
    return x * table[0] + moved * way


def seen_scores(query, near, far, half):
    scale = HD ** (-0.5)
    rows = lax.broadcasted_iota(jnp.int32, (half, half), 0)
    cols = lax.broadcasted_iota(jnp.int32, (half, half), 1)
    own = jnp.where(cols <= rows, dot(query, near, NT) * scale, MASKED)
    peak = jnp.max(own, axis=1, keepdims=True)
    if far is None:
        own = jnp.exp(own - peak)
        return own / jnp.sum(own, axis=1, keepdims=True), None
    before = dot(query, far, NT) * scale
    peak = jnp.maximum(peak, jnp.max(before, axis=1, keepdims=True))
    own, before = jnp.exp(own - peak), jnp.exp(before - peak)
    total = jnp.sum(own, axis=1, keepdims=True) + jnp.sum(before, axis=1, keepdims=True)
    return own / total, before / total


def attend_body(half, skip, x_ref, w_ref, t_ref, out_ref, q_ref, k_ref, v_ref):
    x = x_ref[...]
    raw = [dot(x[skip:], w_ref[0], NN), dot(x, w_ref[1], NN), dot(x, w_ref[2], NN)]
    for h in range(w_ref.shape[2] // HD):
        at = slice(h * HD, (h + 1) * HD)
        query = turned(raw[0][:, at], t_ref[:, skip:], 1.0).astype(BF)
        keys = turned(raw[1][:, at], t_ref[...], 1.0).astype(BF)
        values = raw[2][:, at].astype(BF)
        q_ref[:, at], k_ref[:, at], v_ref[:, at] = query, keys, values
        part = lambda x, g, gone=0: x[g * half - gone : (g + 1) * half - gone]
        for g in range(skip // half, 3):
            own, before = seen_scores(
                part(query, g, skip), part(keys, g), part(keys, 0) if g else None, half
            )
            seen = dot(own.astype(BF), part(values, g), NN)
            if g:
                seen = seen + dot(before.astype(BF), part(values, 0), NN)
            out_ref[g * half - skip : (g + 1) * half - skip, at] = seen.astype(BF)


def head_pairs(inner):
    return 2 * HD if inner % (2 * HD) == 0 else HD


def attention(first_in, weights, tables, half, skip):
    count, width = first_in.shape
    inner = weights.shape[2]
    block = head_pairs(inner)
    columns = lambda rows: pl.BlockSpec((rows, block), lambda h: (0, h))
    shape = lambda rows: jax.ShapeDtypeStruct((rows, inner), BF)
    return pl.pallas_call(
        lambda *refs: attend_body(half, skip, *refs),
        grid=(inner // block,),
        in_specs=[
            pl.BlockSpec((count, width), lambda h: (0, 0)),
            pl.BlockSpec((3, width, block), lambda h: (0, 0, h)),
            pl.BlockSpec(tables.shape, lambda h: (0, 0, 0)),
        ],
        out_specs=[columns(count - skip), columns(count - skip), columns(count), columns(count)],
        out_shape=[shape(count - skip), shape(count - skip), shape(count), shape(count)],
        compiler_params=pltpu.CompilerParams(vmem_limit_bytes=48 * 2**20),
        cost_estimate=LIGHT,
        name="attend",
    )(first_in, weights, tables)


def attend_back_body(half, d_ref, q_ref, k_ref, v_ref, t_ref, out_ref):
    scale = HD ** (-0.5)
    for h in range(d_ref.shape[1] // HD):
        at = slice(h * HD, (h + 1) * HD)
        part = lambda ref, g: ref[g * half : (g + 1) * half, at]
        back_keys = back_values = None
        for g in (1, 2):
            query, far, near = part(q_ref, g), part(k_ref, 0), part(k_ref, g)
            upstream = part(d_ref, g - 1)
            own, before = seen_scores(query, near, far, half)
            own_pull = dot(upstream, part(v_ref, g), NT)
            far_pull = dot(upstream, part(v_ref, 0), NT)
            mean = jnp.sum(own * own_pull, axis=1, keepdims=True) + jnp.sum(
                before * far_pull, axis=1, keepdims=True
            )
            own_back = (own * (own_pull - mean)).astype(BF)
            far_back = (before * (far_pull - mean)).astype(BF)
            back_query = (dot(own_back, near, NN) + dot(far_back, far, NN)) * scale
            rows = slice(g * half, (g + 1) * half)
            out_ref[0, rows, at] = turned(
                back_query, t_ref[:, rows], -1.0
            ).astype(BF)
            out_ref[1, rows, at] = turned(
                dot(own_back, query, TN) * scale, t_ref[:, rows], -1.0
            ).astype(BF)
            out_ref[2, rows, at] = dot(own.astype(BF), upstream, TN).astype(BF)
            more_keys, more_values = dot(far_back, query, TN), dot(before.astype(BF), upstream, TN)
            back_keys = more_keys if back_keys is None else back_keys + more_keys
            back_values = more_values if back_values is None else back_values + more_values
        out_ref[0, :half, at] = jnp.zeros((half, HD), BF)
        out_ref[1, :half, at] = turned(back_keys * scale, t_ref[:, :half], -1.0).astype(BF)
        out_ref[2, :half, at] = back_values.astype(BF)


def attention_back(back_attended, query, keys, values, tables, half):
    count, inner = keys.shape
    block = head_pairs(inner)
    columns = lambda rows: pl.BlockSpec((rows, block), lambda h: (0, h))
    return pl.pallas_call(
        lambda *refs: attend_back_body(half, *refs),
        grid=(inner // block,),
        in_specs=[
            columns(count - half),
            columns(count),
            columns(count),
            columns(count),
            pl.BlockSpec(tables.shape, lambda h: (0, 0, 0)),
        ],
        out_specs=pl.BlockSpec((3, count, block), lambda h: (0, 0, h)),
        out_shape=jax.ShapeDtypeStruct((3, count, inner), BF),
        compiler_params=pltpu.CompilerParams(vmem_limit_bytes=48 * 2**20),
        cost_estimate=LIGHT,
        name="attend_back",
    )(back_attended, query, keys, values, tables)


def hidden_body(skip, before, out_ref, *slope_ref):
    share = 0.5 + 0.5 * lax.erf(before * 0.5**0.5)
    out_ref[...] = (before * share).astype(BF)
    if slope_ref:
        kept = before[skip:]
        bell = jnp.exp(-0.5 * kept * kept) * (2.0 * jnp.pi) ** (-0.5)
        slope_ref[0][...] = share[skip:] + kept * bell


def over_shards(pair, low_ref, x_ref, w_refs, rows_first):
    total = None
    ring = w_refs[0].shape[0]
    slab = w_refs[0].shape[1 if rows_first else 2]
    for side in range(pair):
        for r in range(ring):
            at = pl.multiple_of(shard_of(r, side, low_ref, pair) * slab, slab)
            term = dot(x_ref[:, pl.ds(at, slab)], w_refs[side][r], NN if rows_first else NT)
            total = term if total is None else total + term
    return total


def hidden_units(second_in, expand, skip=None):
    count, width = second_in.shape
    pair = dp_shape()[1]
    if isinstance(expand, tuple) and expand[0].shape[1] % 128:
        expand = rows_of(*expand).reshape(width, -1)
    sides = isinstance(expand, tuple)
    units = expand[0].shape[2] if sides else expand.shape[1]
    block = 256
    column = lambda rows: pl.BlockSpec((rows, block), lambda i, l: (0, i))
    weights = list(expand[:pair]) if sides else [expand]
    weight_specs = [
        pl.BlockSpec(x.shape[:2] + (block,), lambda i, l: (0, 0, i)) if sides else column(width)
        for x in weights
    ]
    out_specs, out_shape = [column(count)], [jax.ShapeDtypeStruct((count, units), BF)]
    if skip is not None:
        out_specs.append(column(count - skip))
        out_shape.append(jax.ShapeDtypeStruct((count - skip, units), F32))

    def body(low_ref, x_ref, *refs):
        w_refs, out_refs = refs[: len(weights)], refs[len(weights) :]
        if sides:
            before = over_shards(pair, low_ref, x_ref, w_refs, True)
        else:
            before = dot(x_ref[...], w_refs[0][...], NN)
        hidden_body(skip, before, *out_refs)

    return pl.pallas_call(
        body,
        grid_spec=pltpu.PrefetchScalarGridSpec(
            num_scalar_prefetch=1,
            grid=(units // block,),
            in_specs=[pl.BlockSpec((count, width), lambda i, l: (0, 0)), *weight_specs],
            out_specs=out_specs,
        ),
        out_shape=out_shape,
        compiler_params=pltpu.CompilerParams(vmem_limit_bytes=48 * 2**20),
        cost_estimate=LIGHT,
        name="hidden",
    )(dp_place()[1].reshape(1), second_in, *weights)


def pull_units(branch_low, weights, slope=None):
    rows, width = branch_low.shape
    pair = dp_shape()[1]
    units, slab = weights[0].shape[1:]
    if slab % 128:
        out = dot(branch_low, columns_of(*weights), NT)
        return (out if slope is None else out * slope).astype(BF)
    block = 256
    weights = list(weights[:pair])
    column = pl.BlockSpec((rows, block), lambda i, l: (0, i))

    def body(low_ref, x_ref, *refs):
        out = over_shards(pair, low_ref, x_ref, refs[:pair], False)
        if slope is not None:
            out = out * refs[pair][...]
        refs[-1][...] = out.astype(BF)

    return pl.pallas_call(
        body,
        grid_spec=pltpu.PrefetchScalarGridSpec(
            num_scalar_prefetch=1,
            grid=(units // block,),
            in_specs=[
                pl.BlockSpec((rows, width), lambda i, l: (0, 0)),
                *(
                    pl.BlockSpec((x.shape[0], block, slab), lambda i, l: (0, i, 0))
                    for x in weights
                ),
                *([] if slope is None else [column]),
            ],
            out_specs=column,
        ),
        out_shape=jax.ShapeDtypeStruct((rows, units), BF),
        compiler_params=pltpu.CompilerParams(vmem_limit_bytes=48 * 2**20),
        cost_estimate=LIGHT,
        name="pull_units",
    )(dp_place()[1].reshape(1), branch_low, *weights, *([] if slope is None else [slope]))


def shard_of(r, side, low, pair):
    return r * pair + (low[0] + side) % pair


def grad_body(x_ref, y_ref, out_ref):
    x = x_ref[...]
    for i in range(y_ref.shape[0]):
        out_ref[0, 0, i] = dot(x, y_ref[i], TN).astype(BF)


def grad_blocks(left, right, sides):
    groups, pair, ring = dp_shape()
    low = dp_place()[1].reshape(1)
    rows = left.shape[0]
    slab = left.shape[1] // groups
    parts, _, width = right.shape
    if slab % 128:
        shards = left.reshape(rows, ring, pair, slab)
        shards = jnp.stack([shards[:, :, (low[0] + s) % pair] for s in sides], axis=2)
        out = jnp.einsum("nrsc,pnw->rspcw", shards, right, preferred_element_type=F32)
        return out.astype(BF)
    first = sides[0]
    return pl.pallas_call(
        lambda low_ref, *refs: grad_body(*refs),
        grid_spec=pltpu.PrefetchScalarGridSpec(
            num_scalar_prefetch=1,
            grid=(ring, len(sides)),
            in_specs=[
                pl.BlockSpec((rows, slab), lambda r, s, l: (0, shard_of(r, s + first, l, pair))),
                pl.BlockSpec(right.shape, lambda r, s, l: (0, 0, 0)),
            ],
            out_specs=pl.BlockSpec(
                (1, 1, parts, slab, width), lambda r, s, l: (r, s, 0, 0, 0)
            ),
        ),
        out_shape=jax.ShapeDtypeStruct((ring, len(sides), parts, slab, width), BF),
        compiler_params=pltpu.CompilerParams(vmem_limit_bytes=48 * 2**20),
        cost_estimate=LIGHT,
        name="grad_blocks",
    )(low, left, right)


def branch_terms(hidden, attended, contract, attend_out, blocks, half):
    groups, pair, ring = dp_shape()
    low = dp_place()[1].reshape(1)
    slab = contract[0].shape[2]
    count = half * len(blocks)
    if slab % 128:
        rows = slice(blocks[0] * half, blocks[0] * half + count)
        out = 0.0
        for x, sides in ((hidden[rows], contract), (attended[rows], attend_out)):
            if pair == 2:
                sides = [by_side(sides[0], sides[1], 1)]
            weight = sides[0].reshape(groups, x.shape[1], slab)
            out = out + jnp.einsum("nf,sfc->nsc", x, weight, preferred_element_type=F32)
        return out.reshape(count, groups * slab).astype(BF)
    weights = [*contract[:pair], *attend_out[:pair]]
    row_block = lambda x, b: pl.BlockSpec((half, x.shape[1]), lambda r, s, l: (b, 0))

    def body(low_ref, *refs):
        x_refs, refs = refs[: 2 * len(blocks)], refs[2 * len(blocks) :]

        def write(side):
            for i in range(len(blocks)):
                refs[-1][i * half : (i + 1) * half] = (
                    dot(x_refs[2 * i][...], refs[side][0], NN)
                    + dot(x_refs[2 * i + 1][...], refs[pair + side][0], NN)
                ).astype(BF)

        for side in range(pair):
            pl.when(pl.program_id(1) == side)(lambda: write(side))

    return pl.pallas_call(
        body,
        grid_spec=pltpu.PrefetchScalarGridSpec(
            num_scalar_prefetch=1,
            grid=(ring, pair),
            in_specs=[
                *(row_block(x, b) for b in blocks for x in (hidden, attended)),
                *(pl.BlockSpec((1,) + x.shape[1:], lambda r, s, l: (r, 0, 0)) for x in weights),
            ],
            out_specs=pl.BlockSpec(
                (count, slab), lambda r, s, l: (0, shard_of(r, s, l, pair))
            ),
        ),
        out_shape=jax.ShapeDtypeStruct((count, groups * slab), BF),
        compiler_params=pltpu.CompilerParams(vmem_limit_bytes=48 * 2**20),
        cost_estimate=LIGHT,
        name="branch",
    )(low, *[hidden, attended] * len(blocks), *weights)


def shard_terms(lefts, weights):
    groups, pair, ring = dp_shape()
    low = dp_place()[1].reshape(1)
    weights = list(weights[:pair])
    count = lefts.shape[1]
    parts, slab, depth = weights[0].shape[1:]
    if slab % 128:
        whole = by_side(weights[0], weights[1], 1) if pair == 2 else weights[0]
        whole = whole.reshape(groups, parts, slab, depth)
        out = jnp.einsum("pnk,gpsk->ngs", lefts, whole, preferred_element_type=F32)
        return out.reshape(count, groups * slab)

    def body(low_ref, x_ref, *refs):
        def write(side):
            total = dot(x_ref[0], refs[side][0, 0], NT)
            for i in range(1, parts):
                total = total + dot(x_ref[i], refs[side][0, i], NT)
            refs[-1][...] = total

        for side in range(pair):
            pl.when(pl.program_id(1) == side)(lambda: write(side))

    return pl.pallas_call(
        body,
        grid_spec=pltpu.PrefetchScalarGridSpec(
            num_scalar_prefetch=1,
            grid=(ring, pair),
            in_specs=[
                pl.BlockSpec(lefts.shape, lambda r, s, l: (0, 0, 0)),
                *(pl.BlockSpec((1,) + x.shape[1:], lambda r, s, l: (r, 0, 0, 0)) for x in weights),
            ],
            out_specs=pl.BlockSpec(
                (count, slab), lambda r, s, l: (0, shard_of(r, s, l, pair))
            ),
        ),
        out_shape=jax.ShapeDtypeStruct((count, groups * slab), F32),
        compiler_params=pltpu.CompilerParams(vmem_limit_bytes=48 * 2**20),
        cost_estimate=LIGHT,
        name="shard_terms",
    )(low, lefts, *weights)


def out_body(x_ref, mine_ref, other_ref, low_ref, unit_ref, low_unit_ref, scale_ref, out_ref):
    mine = pl.program_id(0) == low_ref[0]
    branch = jnp.where(mine, mine_ref[...].astype(F32), other_ref[...].astype(F32))
    out = x_ref[...].astype(F32) + branch
    unit, scale = normalize(out)
    unit_ref[...] = unit
    low_unit_ref[...] = unit.astype(BF)
    scale_ref[...] = scale
    out_ref[...] = out.astype(BF)


def out_rows(x, halves):
    mine, other, low = halves
    rows, width = x.shape
    block = 128
    steps = rows // 2 // block
    whole = pl.BlockSpec((block, width), lambda h, i: (h * steps + i, 0))
    part = pl.BlockSpec((block, width), lambda h, i: (i, 0))
    return pl.pallas_call(
        out_body,
        grid=(2, steps),
        in_specs=[whole, part, part, pl.BlockSpec(memory_space=pltpu.SMEM)],
        out_specs=[whole, whole, pl.BlockSpec((block, 1), lambda h, i: (h * steps + i, 0)), whole],
        out_shape=[
            jax.ShapeDtypeStruct((rows, width), F32),
            jax.ShapeDtypeStruct((rows, width), BF),
            jax.ShapeDtypeStruct((rows, 1), F32),
            jax.ShapeDtypeStruct((rows, width), BF),
        ],
        compiler_params=pltpu.CompilerParams(vmem_limit_bytes=48 * 2**20),
        cost_estimate=LIGHT,
        name="out_rows",
    )(x, mine, other, low)


def pull_body(mine_ref, other_ref, low_ref, weight_ref, unit_ref, scale_ref, out_ref, low_out_ref):
    mine = pl.program_id(0) == low_ref[0]
    upstream = jnp.where(mine, mine_ref[...].astype(F32), other_ref[...].astype(F32))
    out = normalize_back(upstream * weight_ref[...], unit_ref[...], scale_ref[...])
    out_ref[...] = out
    low_out_ref[...] = out.astype(BF)


def pull_rows(halves, weight, unit, scale):
    mine, other, low = halves
    rows, width = unit.shape
    block = 128
    steps = rows // 2 // block
    whole = lambda columns: pl.BlockSpec((block, columns), lambda h, i: (h * steps + i, 0))
    part = pl.BlockSpec((block, width), lambda h, i: (i, 0))
    return pl.pallas_call(
        pull_body,
        grid=(2, steps),
        in_specs=[
            part,
            part,
            pl.BlockSpec(memory_space=pltpu.SMEM),
            whole(1),
            whole(width),
            whole(1),
        ],
        out_specs=[whole(width), whole(width)],
        out_shape=[
            jax.ShapeDtypeStruct((rows, width), F32),
            jax.ShapeDtypeStruct((rows, width), BF),
        ],
        compiler_params=pltpu.CompilerParams(vmem_limit_bytes=48 * 2**20),
        cost_estimate=LIGHT,
        name="pull_rows",
    )(mine, other, low, weight, unit, scale)


def borrow_rows(tail, order, first=(), last=()):
    groups = lax.axis_size("dp")
    parts = lax.axis_size("tensor")
    count, rows, width = tail.shape
    share = rows // parts
    mine = lax.dynamic_slice_in_dim(tail, lax.axis_index("tensor") * share, share, 1)
    mine = mine.reshape(count, groups, share // groups, width).swapaxes(0, 1)
    spread = after(lax.all_to_all(mine, "dp", split_axis=0, concat_axis=0, tiled=True), *first)
    landed = lax.all_to_all(
        jnp.take(spread, order, axis=0), "dp", split_axis=0, concat_axis=0, tiled=True
    )
    landed = landed.swapaxes(0, 1).reshape(count, share, width)
    return tensor_join(after(landed, *last)).swapaxes(0, 1).reshape(count, rows, width)


TILE = 1280
CHUNK = 256
PULL_CHUNK = 640


def head_body(vocab, x_ref, w_ref, t_ref, *refs):
    logits_ref, stats_ref, peak_ref, total_ref, picked_ref = refs if len(refs) == 5 else (None, *refs)
    step = pl.program_id(0)

    @pl.when(step == 0)
    def _():
        peak_ref[...] = jnp.full(peak_ref.shape, MASKED, F32)
        total_ref[...] = jnp.zeros(total_ref.shape, F32)
        picked_ref[...] = jnp.zeros(picked_ref.shape, F32)

    x, target = x_ref[...], t_ref[...]
    lanes = lax.broadcasted_iota(jnp.int32, (x.shape[0], 128), 1)
    for c in range(0, TILE, CHUNK):
        logits = dot(x, w_ref[c : c + CHUNK], NT)
        if logits_ref is not None:
            logits_ref[:, c : c + CHUNK] = logits
        parts = []
        picked = picked_ref[...]
        for d in range(0, CHUNK, 128):
            column = lanes + (step * TILE + c + d)
            part = jnp.where(column < vocab, logits[:, d : d + 128], MASKED)
            picked = picked + jnp.where(column == target, part, 0.0)
            parts.append(part)
        picked_ref[...] = picked
        old = peak_ref[...]
        peak = old
        for part in parts:
            peak = jnp.maximum(peak, part)
        total = total_ref[...] * jnp.exp(old - peak)
        for part in parts:
            total = total + jnp.exp(part - peak)
        peak_ref[...] = peak
        total_ref[...] = total

    @pl.when(step == pl.num_programs(0) - 1)
    def _():
        peak = jnp.max(peak_ref[...], axis=1, keepdims=True)
        total = jnp.sum(total_ref[...] * jnp.exp(peak_ref[...] - peak), axis=1, keepdims=True)
        picked = jnp.sum(picked_ref[...], axis=1, keepdims=True)
        rows = jnp.where(lanes == 0, peak, jnp.where(lanes == 1, total, picked))
        stats_ref[...] = rows.T[:8]


def head_stats(unit_low, table, local_targets, keep):
    rows, width = unit_low.shape
    vocab = table.shape[0]
    tiles = pl.cdiv(vocab, TILE)
    out_specs = [pl.BlockSpec((8, rows), lambda i: (0, 0))]
    out_shape = [jax.ShapeDtypeStruct((8, rows), F32)]
    if keep:
        out_specs.insert(0, pl.BlockSpec((rows, TILE), lambda i: (0, i)))
        out_shape.insert(0, jax.ShapeDtypeStruct((rows, vocab), F32))
    out = pl.pallas_call(
        lambda *refs: head_body(vocab, *refs),
        grid=(tiles,),
        in_specs=[
            pl.BlockSpec((rows, width), lambda i: (0, 0)),
            pl.BlockSpec((TILE, width), lambda i: (i, 0)),
            pl.BlockSpec((rows, 1), lambda i: (0, 0)),
        ],
        out_specs=out_specs,
        out_shape=out_shape,
        scratch_shapes=[pltpu.VMEM((rows, 128), F32)] * 3,
        compiler_params=pltpu.CompilerParams(vmem_limit_bytes=48 * 2**20),
        cost_estimate=LIGHT,
        name="head",
    )(unit_low, table, local_targets[:, None])
    return out[-1][:3], out[0] if keep else None


def head_pull_body(vocab, tiles, x_ref, w_ref, row_ref, t_ref, out_ref, pull_ref, total_ref):
    step = pl.program_id(0)

    @pl.when(step == 0)
    def _():
        total_ref[...] = jnp.zeros(total_ref.shape, F32)

    def add(masked):
        for c in range(0, TILE, PULL_CHUNK):
            at = slice(c, c + PULL_CHUNK)
            column = lax.broadcasted_iota(jnp.int32, (x_ref.shape[0], PULL_CHUNK), 1)
            column = column + (step * TILE + c)
            pull = jnp.where(column == t_ref[...], 1.0, 0.0) - jnp.exp(
                x_ref[:, at] - row_ref[:, 0:1]
            ) * row_ref[:, 1:2]
            if masked:
                pull = jnp.where(column < vocab, pull, 0.0)
            pull_ref[:, at] = pull.astype(BF)
        width = w_ref.shape[1]
        for c in range(0, width, width // 4):
            at = slice(c, c + width // 4)
            weight = w_ref[:, at]
            if masked:
                seen = lax.broadcasted_iota(jnp.int32, weight.shape, 0)
                seen = seen < vocab - (tiles - 1) * TILE
                weight = jnp.where(seen, weight.astype(F32), 0.0).astype(BF)
            total_ref[:, at] += dot(pull_ref[...], weight, NN)

    pl.when(step < tiles - 1)(lambda: add(False))
    pl.when(step == tiles - 1)(lambda: add(True))

    @pl.when(step == tiles - 1)
    def _():
        out_ref[...] = total_ref[...].astype(BF)


def head_pull(logits, table, row, targets):
    rows, vocab = logits.shape
    width = table.shape[1]
    tiles = pl.cdiv(vocab, TILE)
    whole = lambda x: pl.BlockSpec(x, lambda i: (0, 0))
    return pl.pallas_call(
        lambda *refs: head_pull_body(vocab, tiles, *refs),
        grid=(tiles,),
        in_specs=[
            pl.BlockSpec((rows, TILE), lambda i: (0, i)),
            pl.BlockSpec((TILE, width), lambda i: (i, 0)),
            whole((rows, 2)),
            whole((rows, 1)),
        ],
        out_specs=whole((rows, width)),
        out_shape=jax.ShapeDtypeStruct((rows, width), BF),
        scratch_shapes=[pltpu.VMEM((rows, TILE), BF), pltpu.VMEM((rows, width), F32)],
        compiler_params=pltpu.CompilerParams(vmem_limit_bytes=48 * 2**20),
        cost_estimate=LIGHT,
        name="head_pull",
    )(logits, table, row, targets[:, None])


def join_stats(stats):
    every = lax.all_gather(stats, "tensor")
    peak = jnp.max(every[:, 0], axis=0)
    total = jnp.sum(every[:, 1] * jnp.exp(every[:, 0] - peak[None]), axis=0)
    return peak, total, jnp.sum(every[:, 2], axis=0)


def adamw_step(master, first, second, gradient, rate, decay):
    new_first = ADAM_ONE * first + (1.0 - ADAM_ONE) * gradient
    new_second = ADAM_TWO * second + (1.0 - ADAM_TWO) * gradient * gradient
    ratio = (
        new_first
        / (1.0 - ADAM_ONE**STEP)
        / (jnp.sqrt(new_second / (1.0 - ADAM_TWO**STEP)) + ADAM_EPSILON)
    )
    return (master - rate * (ratio + decay * master), new_first, new_second)


def per_device(
    policy_rows,
    frozen_rows,
    next_tokens,
    desirable,
    answer_len,
    partner,
    norms_copy,
    attend_in_copy,
    attend_out_copy,
    expand_copy,
    contract_copy,
    norms_master,
    attend_in_master,
    attend_out_master,
    expand_master,
    contract_master,
    norms_first,
    attend_in_first,
    attend_out_first,
    expand_first,
    contract_first,
    norms_second,
    attend_in_second,
    attend_out_second,
    expand_second,
    contract_second,
    frozen_norms,
    frozen_in,
    frozen_out,
    frozen_expand,
    frozen_contract,
    vocab_table,
):
    groups = lax.axis_size("dp")
    own_index = lax.axis_index("dp")
    half = policy_rows.shape[0] // 2
    inner = attend_in_copy.shape[2]
    slab = attend_in_copy.shape[1]
    width = policy_rows.shape[1]
    inverse = jnp.zeros_like(partner).at[partner].set(jnp.arange(groups, dtype=jnp.int32))
    other_index = partner[own_index]

    norms_full = gather_small(norms_copy).swapaxes(0, 1).reshape(4, width).astype(F32)
    units = expand_copy.shape[1]
    _, pair, ring = dp_shape()
    _, low = dp_place()
    swap = pair_swap if pair == 2 else (lambda value: None)
    cut = (units + inner) // 2
    out_came = swap(attend_out_copy)
    attend_mine = gather_ring(attend_in_copy)
    expand_mine = gather_ring(expand_copy)
    contract_mine = gather_ring(contract_copy)
    out_mine = gather_ring(attend_out_copy)
    out_other = None if out_came is None else gather_ring(out_came)
    norms_full = norms_full if out_came is None else after(norms_full, out_came)

    other = borrow_rows(jnp.stack([frozen_rows[half:], policy_rows[half:]]), partner)
    other, attend_mine = lax.optimization_barrier((other, attend_mine))
    tables = turn_tables(half)

    frozen_work = jnp.concatenate([frozen_rows, other[0]], axis=0).astype(F32)
    frozen_unit, _ = normalize(frozen_work)
    frozen_first_in = (frozen_unit * frozen_norms[0] + frozen_norms[1]).astype(BF)
    frozen_second_in = (frozen_unit[half:] * frozen_norms[2] + frozen_norms[3]).astype(BF)
    frozen_first_in, frozen_second_in, norms_full = lax.optimization_barrier(
        (frozen_first_in, frozen_second_in, norms_full)
    )
    attend_other = swap(attend_mine)
    frozen_attended = attention(frozen_first_in, frozen_in, tables, half, half)[0]
    (frozen_hidden,) = hidden_units(frozen_second_in, frozen_expand)
    frozen_part = dot(frozen_attended, frozen_out, NN) + dot(frozen_hidden, frozen_contract, NN)
    frozen_part, attend_other, expand_mine = lax.optimization_barrier(
        (frozen_part.astype(BF), attend_other, expand_mine)
    )
    expand_other = swap(expand_mine)
    frozen_low = out_rows(
        jnp.concatenate([frozen_rows[half:], other[0]], axis=0), tensor_halves(frozen_part)
    )[1]
    vocab_local = vocab_table.shape[1]
    table = vocab_table.T
    targets = (
        jnp.concatenate([next_tokens[own_index], next_tokens[other_index]])
        - lax.axis_index("tensor") * vocab_local
    )
    targets = jnp.where((targets >= 0) & (targets < vocab_local), targets, -1)
    work = jnp.concatenate([policy_rows, other[1]], axis=0).astype(F32)
    unit, inverse_scale = normalize(work)
    first_in = (unit * norms_full[0] + norms_full[1]).astype(BF)
    second_in = (unit * norms_full[2] + norms_full[3]).astype(BF)
    attend_in = rows_of(attend_mine, attend_other)
    attend_in = attend_in.swapaxes(0, 1).reshape(3, width, inner)
    attended, query, keys, values = attention(first_in, attend_in, tables, half, 0)
    second_in, contract_mine, attended, expand_other = lax.optimization_barrier(
        (second_in, contract_mine, attended, expand_other)
    )
    contract_other = swap(contract_mine)
    frozen_low, second_in = lax.optimization_barrier((frozen_low, second_in))
    frozen_stats, _ = head_stats(frozen_low, table, targets, False)
    frozen_peak, frozen_total, frozen_picked = join_stats(frozen_stats)
    second_in, frozen_peak = lax.optimization_barrier((second_in, frozen_peak))
    hidden, slope_units = hidden_units(second_in, (expand_mine, expand_other), half)

    contract, attend_out = (contract_mine, contract_other), (out_mine, out_other)
    scored_halves = tensor_halves(
        branch_terms(hidden, attended, contract, attend_out, (1, 2), half)
    )
    unit_out, unit_low, inverse_out, out_low = out_rows(
        jnp.concatenate([policy_rows[half:], other[1]], axis=0), scored_halves
    )
    stats, logits = head_stats(unit_low, table, targets, True)
    peak, total, picked = join_stats(stats)
    log_chance = jnp.stack(
        [picked - peak - jnp.log(total), frozen_picked - frozen_peak - jnp.log(frozen_total)]
    )
    steps = jnp.arange(half, dtype=jnp.int32)
    own_count = answer_len[own_index]
    other_count = answer_len[other_index]
    own_live = (steps < own_count).astype(F32)
    other_live = (steps < other_count).astype(F32)
    own_total = own_count.astype(F32)
    other_total = other_count.astype(F32)
    own_mean = jnp.sum(log_chance[:, :half] * own_live, axis=1) / own_total
    other_mean = jnp.sum(log_chance[:, half:] * other_live, axis=1) / other_total
    gaps = jnp.stack([own_mean[0] - own_mean[1], other_mean[0] - other_mean[1]])
    row = jnp.stack([peak, 1.0 / total], axis=1)
    back_part = head_pull(logits, table, row, targets)
    if lax.axis_size("tensor") == 4:
        back_part = tensor_near(back_part)
    every = gather_small(after(gaps, back_part))
    drift = jnp.sum(every[:, 1]) / groups
    sign = (2 * desirable - 1).astype(F32)
    settled = jax.nn.sigmoid(KTO_BETA * sign * (every[:, 0] - jax.nn.softplus(drift)))
    slope = KTO_BETA * sign * settled * (1.0 - settled)
    loss_total = jnp.sum(1.0 - settled)
    pull = jnp.sum(slope) * jax.nn.sigmoid(drift) / groups
    row_weight = jnp.concatenate(
        [-slope[own_index] * own_live / own_total, pull * other_live / other_total]
    )

    if lax.axis_size("tensor") == 4:
        back_part = after(tensor_far(back_part), row_weight)
        side_row = (lax.axis_index("tensor") % 2).reshape(1)
        back_sum = (back_part, tensor_swap(back_part, 1), side_row)
    else:
        back_sum = tensor_halves(back_part)
    back_out, branch_low = pull_rows(back_sum, row_weight[:, None], unit_out, inverse_out)

    features_scored = jnp.concatenate([hidden[half:], attended[half:]], axis=1)
    near_features, far_features = features_scored[:, :cut][None], features_scored[:, cut:][None]
    near_sent = grad_blocks(branch_low, near_features, (1,))
    near_came = swap(near_sent)
    branch_low = after(branch_low, near_sent)
    far_blocks = grad_blocks(branch_low, far_features, range(pair))
    far_back = scatter_ring(far_blocks)

    branch_low = after(branch_low, far_blocks)
    back_expand = pull_units(branch_low, contract, slope_units)
    expand_sent = grad_blocks(second_in[half:], back_expand[None], (1,))
    near_kept = grad_blocks(after(branch_low, expand_sent), near_features, (0,))
    near_ring = to_ring(near_kept, near_came)
    grad_near = scatter_ring(near_ring)[0].astype(F32)

    expand_sent, branch_low, back_expand, near_ring = lax.optimization_barrier(
        (expand_sent, branch_low, back_expand, near_ring)
    )
    expand_came = swap(expand_sent)
    back_attended = pull_units(branch_low, attend_out)
    back_three = attention_back(back_attended, query, keys, values, tables, half)
    attend_sent = grad_blocks(first_in, back_three, (1,))
    sided = lambda sides: [x if x is None else x[:, None] for x in sides]
    back_second = shard_terms(back_expand[None], sided((expand_mine, expand_other)))
    back_first = shard_terms(back_three, (attend_mine, attend_other))

    unit_scored = unit[half:]
    grad_norms = sum_small(
        jnp.stack(
            [
                jnp.sum(back_first * unit, axis=0),
                jnp.sum(back_first, axis=0),
                jnp.sum(back_second * unit_scored, axis=0),
                jnp.sum(back_second, axis=0),
            ]
        ),
        ("tensor",),
    )
    back_h = back_first * norms_full[0] + jnp.pad(
        back_second * norms_full[2], ((half, 0), (0, 0))
    )
    four = lax.axis_size("tensor") == 4
    back_h = tensor_near(back_h) if four else lax.psum(back_h.astype(BF), "tensor")
    second_scored, far_back = lax.optimization_barrier(
        (second_in[half:], far_back, attend_sent, back_h)
    )[:2]
    expand_kept = grad_blocks(second_scored, back_expand[None], (0,))
    expand_ring = to_ring(expand_kept, expand_came)
    expand_back = scatter_ring(expand_ring)

    attend_sent, back_three, expand_ring = lax.optimization_barrier(
        (attend_sent, back_three, expand_ring)
    )
    attend_came = swap(attend_sent)
    attend_kept = grad_blocks(after(first_in, expand_ring), back_three, (0,))
    attend_ring = to_ring(attend_kept, attend_came)
    across = tensor_swap(back_h, 2) if four else back_h
    attend_ring, expand_back, across = lax.optimization_barrier((attend_ring, expand_back, across))
    if four:
        back_h = (back_h.astype(F32) + across.astype(F32)).astype(BF)
        low_row = (lax.axis_index("tensor") % 2).reshape(1)
        back_h = whole_rows(back_h, tensor_swap(back_h, 1), low_row)
    grad_expand = expand_back[0].astype(F32)
    attend_back = scatter_ring(attend_ring)
    hidden = after(hidden, attend_ring)
    back_work = normalize_back(
        back_h.astype(F32), unit, inverse_scale
    ) + jnp.pad(back_out, ((half, 0), (0, 0)))
    out_prompt = work[:half] + tensor_sum(
        branch_terms(hidden, attended, contract, attend_out, (0,), half)
    ).astype(F32)
    mixed = jnp.concatenate([out_prompt.astype(BF), out_low[:half]], axis=0)
    grad_norms = sum_small(after(grad_norms, attend_ring), ("dp",))
    grad_norms = lax.dynamic_slice_in_dim(grad_norms, own_index * slab, slab, 1)
    returned = borrow_rows(back_work[None, 2 * half :].astype(BF), inverse, (attend_ring,), (attend_back,))[0]
    grad_far = far_back[0, 0].astype(F32)
    if pair == 2:
        grad_far = grad_far + pair_swap(after(far_back[1, 0], attend_ring)).astype(F32)
    grad_join = jnp.concatenate([grad_near.T, grad_far.T], axis=0)
    grad_contract, grad_attend_out = grad_join[:units], grad_join[units:]
    input_grad = jnp.concatenate(
        [back_work[:half], back_work[half : 2 * half] + returned.astype(F32)], axis=0
    )

    matrix_rate = 0.5 * D ** (-0.5)
    out_rate = 0.5 * max(D // HALF, 1) ** (-0.5)
    masters = (norms_master, attend_in_master, attend_out_master, expand_master, contract_master)
    firsts = (norms_first, attend_in_first, attend_out_first, expand_first, contract_first)
    seconds = (norms_second, attend_in_second, attend_out_second, expand_second, contract_second)
    rates = (NORM_RATE, matrix_rate, out_rate, matrix_rate, matrix_rate)
    decays = (0.0, DECAY_RATE, DECAY_RATE, DECAY_RATE, DECAY_RATE)
    gradients = [grad_norms, None, grad_attend_out, grad_expand, grad_contract]
    updated = [None] * 5
    for i in (2, 4, 3, 0):
        updated[i] = adamw_step(
            masters[i], firsts[i], seconds[i], gradients[i], rates[i], decays[i]
        )
    attend_back, *waited = lax.optimization_barrier(
        (attend_back, *(updated[i][0] for i in (2, 4, 3, 0)))
    )
    for i, first in zip((2, 4, 3, 0), waited):
        updated[i] = (first,) + updated[i][1:]
    updated[1] = adamw_step(
        masters[1], firsts[1], seconds[1], attend_back.astype(F32), rates[1], decays[1]
    )
    return (
        mixed,
        input_grad,
        jnp.reshape(loss_total, (1,)),
        *(step[0] for step in updated),
        *(step[1] for step in updated),
        *(step[2] for step in updated),
    )


def solution(mesh):
    rows = P("dp", None)
    all_of = P()
    state = (P(None, "dp"), P(None, "dp", "tensor"), P("tensor", "dp"), P("dp", "tensor"), P("tensor", "dp"))
    frozen = (all_of, P(None, None, "tensor"), P("tensor", None), P(None, "tensor"), P("tensor", None))
    return jax.shard_map(
        per_device,
        mesh=mesh,
        in_specs=(rows, rows) + (all_of,) * 4 + state * 4 + frozen + (P(None, "tensor"),),
        out_specs=(rows, rows, all_of) + state * 3,
        check_vma=False,
    )
```
